32 devices in a mesh: group: 2 (over y), expert: 4 (over z), dp: 4 (over x, core).
Axes of the slice: x: 2, y: 2, z: 4, core: 2. Of those that a mesh axis runs over, the one named last changes fastest.
Arguments:
- tokens: bfloat16 [1024, 3072], P(('group', 'expert'), 'dp'), parts along dimension 0, may hold values from -6 to 6
- cotangent: bfloat16 [1024, 3072], P(('group', 'expert'), 'dp'), parts along dimension 0, may hold values from -6 to 6
- routes: int32 [1024, 2], P(('group', 'expert')), parts along dimension 0, may hold values from 0 to 3, all different within a row; in each aligned block of 128 rows (0 to 127, 128 to 255, ...) at most 74 rows name the same one
- route_gates: float32 [1024, 2], P(('group', 'expert')), parts along dimension 0, may hold values from 0.1 to 1
- gate_weight: bfloat16 [4, 3072, 768], P('expert', 'dp'), may hold values from -0.109375 to 0.109375
- up_weight: bfloat16 [4, 3072, 768], P('expert', 'dp'), may hold values from -0.109375 to 0.109375
- down_weight: bfloat16 [4, 768, 3072], P('expert', None, 'dp'), may hold values from -0.21875 to 0.21875
Outputs:
- mixed: bfloat16 [1024, 3072], P(('group', 'expert'), 'dp'), parts along dimension 0
- grad_tokens: bfloat16 [1024, 3072], P(('group', 'expert'), 'dp'), parts along dimension 0
- grad_gates: float32 [1024, 2], P(('group', 'expert')), parts along dimension 0
- grad_gate_weight: bfloat16 [8, 3072, 768], P(('group', 'expert'), 'dp'), parts along dimension 0
- grad_up_weight: bfloat16 [8, 3072, 768], P(('group', 'expert'), 'dp'), parts along dimension 0
- grad_down_weight: bfloat16 [8, 768, 3072], P(('group', 'expert'), None, 'dp'), parts along dimension 0
The draws below stay inside these ranges and needn't reach their ends.
There are 2 independent parts, one for each index of `group`. The reference program is written for one: setup_inputs(seed, part) draws one part's arguments, and reference() takes and returns one part's arrays. A program takes and returns all parts, laid end to end along the dimension named above; an argument that names none is the same for every part. Nothing has to cross between parts.
Inputs may be any that keep to these rules, and one draw needn't show every extreme that they name: `routes`: each row names 2 different experts. Among the 128 tokens of one index of expert no expert is named more than 74 times, and in some such block of tokens some expert is named exactly 74 times.
All inputs are finite; a program needn't handle non-finite values.
Results may differ from the reference program's by a relative error of at most 0.019.
Values may be sent and summed in bfloat16 or wider, within the bound.
No kernel may reach another device: no remote copies, remote signals or barrier semaphores. Data moves between devices by JAX's collectives and lax.ppermute only.
A program may use at most 64 MiB of HBM per device.

```python
import math
import jax
import jax.numpy as jnp
import numpy as np
from jax import lax

D = 3072
FF = 768
TOK_DEV = 128
EXPERTS = 4
TOP = 2
CAP = 74
SLOTS = 296
TOKENS = 512
D_BLOCK = 768
N_EXPERT = 4
N_DP = 4


def levels(key, extent, cuts, smallest, largest):
    def one(axis_at, blocks):
        heights = jax.random.uniform(jax.random.fold_in(jax.random.fold_in(key, 6), axis_at), (blocks,), jnp.float32, smallest / len(cuts), largest / len(cuts))
        return jnp.repeat(jnp.exp(heights), extent[axis_at] // blocks).reshape((-1,) + (1,) * (len(extent) - axis_at - 1))

    level = one(*cuts[0])
    for cut in cuts[1:]:
        level = level * one(*cut)
    return level


def routed_block(stream_key, own, number, rows, number_of, top, bound, slope):
    sequence = jax.random.permutation(stream_key, number_of)
    crowded, ordinary = load_shares(number_of, rows * top, bound, slope, True), load_shares(number_of, rows * top, bound, slope, False)
    places = jnp.arange(number_of)

    def named(tallies, rotation):
        used = int((tallies > 0).sum())
        fixed = max(1, used // 4)
        moved = fixed + (places - fixed + rotation * (used - fixed)) % max(1, number_of - fixed)
        return jnp.zeros((number_of,), jnp.int32).at[sequence[jnp.where(places < fixed, places, moved)]].set(jnp.asarray(tallies, jnp.int32))

    tallies = jnp.where(number % 4 == 0, named(crowded, number // 4), named(ordinary, number - number // 4 - 1))
    mixed = jax.random.permutation(jax.random.fold_in(own, 3), number_of)
    source_of, sink = mixed[0:number_of // 2 * 2:2], mixed[1:number_of // 2 * 2:2]
    room = jnp.minimum(tallies[source_of] - 1, bound - tallies[sink]) // 2
    room = jnp.where((source_of == sequence[0]) | (sink == sequence[0]) | (tallies[sink] == 0), 0, jnp.maximum(room, 0))
    moved = jax.random.randint(jax.random.fold_in(own, 4), (number_of // 2,), 0, 1 << 20) % (room + 1)
    tallies = tallies.at[source_of].add(-moved).at[sink].add(moved)
    labels = jnp.searchsorted(jnp.cumsum(tallies), jnp.arange(rows * top), side="right").astype(jnp.int32)
    table = labels.reshape(top, rows).T
    table = table[jax.random.permutation(jax.random.fold_in(own, 1), rows)]
    rotation = jax.random.randint(jax.random.fold_in(own, 2), (rows, 1), 0, top)
    return jnp.take_along_axis(table, (jnp.arange(top)[None, :] + rotation) % top, axis=1)


def load_shares(count, total, limit, slope, full):
    weights = [(1 << 20) // math.isqrt(standing ** slope) + 1 for standing in range(1, count + 1)]
    largest = limit if full else min(limit, max(-(-total // count), total * weights[0] // sum(weights)))
    least = 1 if total - largest >= count - 1 else 0
    given, spare = [largest] + [least] * (count - 1), total - largest - least * (count - 1)
    while spare > 0:
        movable = [i for i in range(1, count) if given[i] < largest] or [i for i in range(1, count) if given[i] < limit]
        mass, left = sum([weights[i] for i in movable]), spare
        for i in movable:
            addition = min(limit - given[i], max(1, left * weights[i] // mass), spare)
            given[i] = given[i] + addition
            spare = spare - addition
    return np.array(given)


def normal_values(stream_key, extent, width, bound, pieces=(), kind=jnp.bfloat16):
    factor_of = levels(stream_key, extent, pieces, -0.22, 0.18) if pieces else 1.0
    drawn = jax.random.normal(stream_key, extent, jnp.float32) * width * factor_of
    return jnp.minimum(jnp.maximum(drawn, -bound), bound).astype(kind)


def setup_inputs(seed: int = 0, part: int = 0) -> dict:
    key_of = jax.random.split(jax.random.key(seed), 8)
    part_splits = jax.random.split(jax.random.fold_in(key_of[7], part), 8)
    tokens = normal_values(part_splits[0], (TOKENS, D), 1.0, 6.0, ((0, 4), (1, 4)))
    cotangent = normal_values(part_splits[1], (TOKENS, D), 1.0, 6.0, ((0, 4), (1, 4)))
    routes_keys = jax.random.split(jax.random.fold_in(part_splits[2], 1), TOKENS // TOK_DEV)
    routes_turns = jax.random.permutation(jax.random.fold_in(part_splits[2], 3), TOKENS // TOK_DEV)
    routes = jax.vmap(lambda own, number: routed_block(jax.random.fold_in(part_splits[2], 2), own, number, TOK_DEV, EXPERTS, TOP, CAP, 2))(routes_keys, routes_turns).reshape((TOKENS, TOP))
    route_gates = jnp.clip(jnp.exp(math.log(1.0) - 2.3025851 * jax.random.uniform(part_splits[3], (TOKENS, TOP), jnp.float32) ** levels(part_splits[3], (TOKENS, TOP), ((0, 4),), -0.2, 0.2)), 0.1, 1.0)
    gate_weight = normal_values(key_of[4], (EXPERTS, D, FF), D ** -0.5, 0.109375, ((0, 4), (1, 4)))
    up_weight = normal_values(key_of[5], (EXPERTS, D, FF), D ** -0.5, 0.109375, ((0, 4), (1, 4)))
    down_weight = normal_values(key_of[6], (EXPERTS, FF, D), FF ** -0.5, 0.21875, ((0, 4), (2, 4)))
    return dict(tokens=tokens, cotangent=cotangent, routes=routes, route_gates=route_gates, gate_weight=gate_weight, up_weight=up_weight, down_weight=down_weight)


def slot_table(routes):
    blocks = routes.reshape(N_EXPERT, TOK_DEV * TOP)
    onehot = (blocks[:, :, None] == jnp.arange(EXPERTS, dtype=jnp.int32)[None, None, :]).astype(jnp.int32)
    before = jnp.cumsum(onehot, axis=1) - onehot
    rank = jnp.sum(before * onehot, axis=2)
    source = jnp.arange(N_EXPERT, dtype=jnp.int32)[:, None]
    return (source * CAP + rank).reshape(-1).astype(jnp.int32)


def block_sum(terms):
    rounded = lax.optimization_barrier(terms.astype(jnp.bfloat16))
    return jnp.sum(rounded.astype(jnp.float32), axis=0)


def reference(tokens, cotangent, routes, route_gates, gate_weight, up_weight, down_weight):
    route_count = TOKENS * TOP
    flat_routes = routes.reshape(-1).astype(jnp.int32)
    places = slot_table(routes)
    owners = jnp.arange(route_count, dtype=jnp.int32) // TOP
    table = jnp.full((EXPERTS, SLOTS), route_count, jnp.int32)
    table = table.at[flat_routes, places].set(jnp.arange(route_count, dtype=jnp.int32))
    scaled = (route_gates.reshape(-1)[:, None] * cotangent[owners].astype(jnp.float32)).astype(jnp.bfloat16)
    zero_row = jnp.zeros((1, D), jnp.bfloat16)
    route_inputs = jnp.concatenate([tokens[owners], zero_row], axis=0)
    route_grads = jnp.concatenate([scaled, zero_row], axis=0)

    def one_expert(index):
        rows = table[index]
        expert_in = route_inputs[rows]
        expert_cot = route_grads[rows]
        split_in = expert_in.astype(jnp.float32).reshape(SLOTS, N_DP, D_BLOCK)
        split_cot = expert_cot.astype(jnp.float32).reshape(SLOTS, N_DP, D_BLOCK)
        gate_blocks = gate_weight[index].astype(jnp.float32).reshape(N_DP, D_BLOCK, FF)
        up_blocks = up_weight[index].astype(jnp.float32).reshape(N_DP, D_BLOCK, FF)
        down_blocks = down_weight[index].astype(jnp.float32).reshape(FF, N_DP, D_BLOCK)
        gate_sum = block_sum(jnp.einsum("rpd,pdf->prf", split_in, gate_blocks))
        up_sum = block_sum(jnp.einsum("rpd,pdf->prf", split_in, up_blocks))
        sigma = jax.nn.sigmoid(gate_sum)
        silu_value = gate_sum * sigma
        hidden = (silu_value * up_sum).astype(jnp.bfloat16)
        expert_out = jnp.dot(hidden, down_weight[index], preferred_element_type=jnp.float32).astype(jnp.bfloat16)
        dhidden = block_sum(jnp.einsum("rpd,fpd->prf", split_cot, down_blocks))
        dgate = (dhidden * up_sum * sigma * (1.0 + gate_sum * (1.0 - sigma))).astype(jnp.bfloat16)
        dup = (dhidden * silu_value).astype(jnp.bfloat16)
        grad_gate = jnp.dot(expert_in.T, dgate, preferred_element_type=jnp.float32).astype(jnp.bfloat16)
        grad_up = jnp.dot(expert_in.T, dup, preferred_element_type=jnp.float32).astype(jnp.bfloat16)
        grad_down = jnp.dot(hidden.T, expert_cot, preferred_element_type=jnp.float32).astype(jnp.bfloat16)
        expert_dx = (jnp.dot(dgate, gate_weight[index].T, preferred_element_type=jnp.float32)
                     + jnp.dot(dup, up_weight[index].T, preferred_element_type=jnp.float32)).astype(jnp.bfloat16)
        return expert_out, expert_dx, grad_gate, grad_up, grad_down

    outputs = lax.map(one_expert, jnp.arange(EXPERTS, dtype=jnp.int32))
    expert_out, expert_dx, grad_gate, grad_up, grad_down = outputs
    back_out = expert_out[flat_routes, places].astype(jnp.float32).reshape(TOKENS, TOP, D)
    back_dx = expert_dx[flat_routes, places].astype(jnp.float32).reshape(TOKENS, TOP, D)
    mixed = jnp.sum(route_gates[:, :, None] * back_out, axis=1).astype(jnp.bfloat16)
    grad_tokens = jnp.sum(back_dx, axis=1).astype(jnp.bfloat16)
    grad_gates = jnp.sum(back_out * cotangent.astype(jnp.float32)[:, None, :], axis=2)
    return mixed, grad_tokens, grad_gates, grad_gate, grad_up, grad_down
```

```python
import functools

import jax
import jax.numpy as jnp
from jax import lax
from jax.experimental import pallas as pl
from jax.experimental.pallas import tpu as pltpu
from jax.sharding import PartitionSpec as P

BF = jnp.bfloat16
F32 = jnp.float32
VMEM_BYTES = 40 * 1024 * 1024


def swap(block, axis, offset):
    count = lax.axis_size(axis)
    return lax.ppermute(block, axis, [(i, i ^ offset) for i in range(count)])


def dot(a, b):
    return lax.dot_general(a, b, (((1,), (0,)), ((), ())), preferred_element_type=F32)


def dot_nt(a, b):
    return lax.dot_general(a, b, (((1,), (1,)), ((), ())), preferred_element_type=F32)


def dot_tn(a, b):
    return lax.dot_general(a, b, (((0,), (0,)), ((), ())), preferred_element_type=F32)


def call(kernel, name, outs, args, scalars=1, scratch=(), flops=0):
    smem = pl.BlockSpec(memory_space=pltpu.SMEM)
    vmem = pl.BlockSpec(memory_space=pltpu.VMEM)
    moved = sum(a.size * a.dtype.itemsize for a in args) + sum(
        o.size * o.dtype.itemsize for o in outs
    )
    return pl.pallas_call(
        kernel,
        name=name,
        out_shape=outs,
        in_specs=[smem] * scalars + [vmem] * (len(args) - scalars),
        out_specs=[vmem] * len(outs),
        scratch_shapes=list(scratch),
        compiler_params=pltpu.CompilerParams(vmem_limit_bytes=VMEM_BYTES),
        cost_estimate=pl.CostEstimate(flops=flops, bytes_accessed=moved, transcendentals=0),
    )(*args)


def chosen(routes, gates, expert):
    hit = routes == expert
    taken = jnp.sum(hit.astype(F32), axis=0, keepdims=True)
    gate = jnp.sum(jnp.where(hit, gates, 0.0), axis=0, keepdims=True)
    return taken, gate


def pack_kernel(peers, me_ref, routes_ref, gates_ref, tokens_ref, cot_ref, *out_refs):
    x_refs, c_refs, place_ref = out_refs[:peers], out_refs[peers : 2 * peers], out_refs[2 * peers]
    me = me_ref[0]
    routes, gates = routes_ref[...], gates_ref[...]
    count = routes.shape[1]
    rows = x_refs[0].shape[0]
    earlier = (
        lax.broadcasted_iota(jnp.int32, (count, count), 0)
        < lax.broadcasted_iota(jnp.int32, (count, count), 1)
    ).astype(BF)
    pairs = [chosen(routes, gates, me ^ j) for j in range(peers)]
    taken = jnp.concatenate([p[0] for p in pairs], axis=0)
    rank = dot(taken.astype(BF), earlier)
    rank = jnp.where(taken > 0.0, rank, -1.0).astype(jnp.int32)
    slot = lax.broadcasted_iota(jnp.int32, (rows, count), 0)
    for j in range(peers):
        place_ref[j * rows : (j + 1) * rows, :] = (slot == rank[j : j + 1]).astype(F32).astype(BF)
    tokens = tokens_ref[...]
    for j in range(peers):
        x_refs[j][...] = dot(place_ref[j * rows : (j + 1) * rows, :], tokens).astype(BF)
    cot = cot_ref[...]
    for j in range(peers):
        place = place_ref[j * rows : (j + 1) * rows, :]
        scale = jnp.sum(place.astype(F32) * pairs[j][1], axis=1, keepdims=True)
        c_refs[j][...] = (dot(place, cot) * scale).astype(BF)


def up_kernel(peers, half_ref, *refs):
    x_refs, (gate_ref, up_ref, keep_ref, send_ref) = refs[:peers], refs[peers:]
    half = half_ref[0]
    width = gate_ref.shape[1]
    x = jnp.concatenate([r[...] for r in x_refs], axis=0)
    rows = x.shape[0] // 2
    for i, w_ref in enumerate((gate_ref, up_ref)):
        y = dot(x, w_ref[...]).astype(BF)
        lanes = slice(i * width, (i + 1) * width)

        @pl.when(half == 0)
        def _():
            keep_ref[:, lanes] = y[:rows]
            send_ref[:, lanes] = y[rows:]

        @pl.when(half == 1)
        def _():
            keep_ref[:, lanes] = y[rows:]
            send_ref[:, lanes] = y[:rows]


def back_kernel(peers, half_ref, *refs):
    c_refs, (down_ref, keep_ref, send_ref) = refs[:peers], refs[peers:]
    half = half_ref[0]
    c = jnp.concatenate([r[...] for r in c_refs], axis=0)
    rows = c.shape[0] // 2
    y = dot_nt(c, down_ref[...]).astype(BF)

    @pl.when(half == 0)
    def _():
        keep_ref[...] = y[:rows]
        send_ref[...] = y[rows:]

    @pl.when(half == 1)
    def _():
        keep_ref[...] = y[rows:]
        send_ref[...] = y[:rows]


def out_kernel(peers, half_ref, mine_ref, other_ref, down_ref, *refs):
    out_refs, (hidden_ref, sums_ref) = refs[:peers], refs[peers:]
    half = half_ref[0]
    width = down_ref.shape[0]
    sums_ref[half] = mine_ref[...]
    sums_ref[1 - half] = other_ref[...]
    rows = mine_ref.shape[0]
    for h in range(2):
        g = sums_ref[h, :, :width].astype(F32)
        u = sums_ref[h, :, width:].astype(F32)
        hidden_ref[h * rows : (h + 1) * rows, :] = (g * jax.nn.sigmoid(g) * u).astype(BF)
    out = dot(hidden_ref[...], down_ref[...]).astype(BF)
    cp = out_refs[0].shape[0]
    for j in range(peers):
        out_refs[j][...] = out[j * cp : (j + 1) * cp]


def dx_kernel(peers, cap, half_ref, sums_ref, hidden_ref, mine_ref, other_ref, gate_ref, up_ref, *refs):
    dx_refs, (dgate_ref, dup_ref, dh_ref, dot_ref) = refs[:peers], refs[peers:]
    half = half_ref[0]
    width = gate_ref.shape[1]
    dh_ref[half] = mine_ref[...]
    dh_ref[1 - half] = other_ref[...]
    rows = mine_ref.shape[0]
    for h in range(2):
        part = slice(h * rows, (h + 1) * rows)
        g = sums_ref[h, :, :width].astype(F32)
        u = sums_ref[h, :, width:].astype(F32)
        dh = dh_ref[h].astype(F32)
        s = jax.nn.sigmoid(g)
        dgate_ref[part, :] = (dh * u * s * (1.0 + g * (1.0 - s))).astype(BF)
        dup_ref[part, :] = (dh * (g * s)).astype(BF)
        dot_ref[part, :] = jnp.sum(hidden_ref[part, :].astype(F32) * dh, axis=1, keepdims=True)
    dx = dot_nt(dgate_ref[...], gate_ref[...]) + dot_nt(dup_ref[...], up_ref[...])
    cp = dx_refs[0].shape[0]
    lanes = 128 * (-(-cp // 128))
    eye = lax.broadcasted_iota(jnp.int32, (cp, lanes), 0) == lax.broadcasted_iota(
        jnp.int32, (cp, lanes), 1
    )
    row = lax.broadcasted_iota(jnp.int32, (cp, lanes), 0)
    for j in range(peers):
        block = dx[j * cp : (j + 1) * cp]
        dx_refs[j][...] = block.astype(BF)
        dots = jnp.sum(jnp.where(eye, dot_ref[j * cp : (j + 1) * cp, :], 0.0), axis=0, keepdims=True)
        high = dots.astype(BF).astype(F32)
        middle = (dots - high).astype(BF).astype(F32)
        low = dots - high - middle
        first = jnp.where(row == cap, high, block[:, :lanes])
        first = jnp.where(row == cap + 1, middle, first)
        first = jnp.where(row == cap + 2, low, first)
        dx_refs[j][:, :lanes] = first.astype(BF)


def grad_kernel(peers, *refs):
    x_refs, c_refs = refs[:peers], refs[peers : 2 * peers]
    hidden_ref, dgate_ref, dup_ref, gg_ref, gu_ref, gd_ref = refs[2 * peers :]
    x = jnp.concatenate([r[...] for r in x_refs], axis=0)
    gg_ref[...] = dot_tn(x, dgate_ref[...]).astype(BF)
    gu_ref[...] = dot_tn(x, dup_ref[...]).astype(BF)
    c = jnp.concatenate([r[...] for r in c_refs], axis=0)
    gd_ref[...] = dot_tn(hidden_ref[...], c).astype(BF)


def merge_kernel(peers, cap, me_ref, routes_ref, gates_ref, place_ref, *refs):
    out_refs, dx_refs = refs[:peers], refs[peers : 2 * peers]
    mixed_ref, grad_ref, gates_out_ref = refs[2 * peers :]
    me = me_ref[0]
    routes, gates = routes_ref[...], gates_ref[...]
    cp = out_refs[0].shape[0]
    highs, lows = [], []
    total = jnp.zeros(gates.shape, F32)
    base = cap // 16 * 16
    for j in range(peers):
        place = place_ref[j * cp : (j + 1) * cp, :]
        _, gate = chosen(routes, gates, me ^ j)
        high = gate.astype(BF).astype(F32)
        highs.append((place.astype(F32) * high).astype(BF))
        lows.append((place.astype(F32) * (gate - high)).astype(BF))
        found = dot(dx_refs[j][base:cp, :cp], place)
        at = cap - base
        value = found[at : at + 1] + found[at + 1 : at + 2] + found[at + 2 : at + 3]
        total = total + jnp.where(routes == (me ^ j), value, 0.0)
    gates_out_ref[...] = total / gates
    out = jnp.concatenate([r[...] for r in out_refs], axis=0)
    mixed = dot_tn(jnp.concatenate(highs, axis=0), out) + dot_tn(jnp.concatenate(lows, axis=0), out)
    mixed_ref[...] = mixed.astype(BF)
    dx = jnp.concatenate([r[...] for r in dx_refs], axis=0)
    grad_ref[...] = dot_tn(place_ref[...], dx).astype(BF)


def added(a, b):
    return (a.astype(F32) + b.astype(F32)).astype(BF)


def reduced(keep, send, dp_count):
    total = added(keep, swap(send, "dp", 1))
    bit = 2
    while bit < dp_count:
        total = added(total, swap(total, "dp", bit))
        bit *= 2
    return total, swap(total, "dp", 1)


def shards(tokens, cotangent, routes, route_gates, gate_weight, up_weight, down_weight):
    peers = lax.axis_size("expert")
    dp_count = lax.axis_size("dp")
    count, top = routes.shape
    width = tokens.shape[1]
    ff = gate_weight.shape[2]
    cap = 7 * count * top // (6 * peers)
    cp = -(-(cap + 3) // 16) * 16
    rows = peers * cp
    gate_w, up_w, down_w = gate_weight[0], up_weight[0], down_weight[0]
    me = lax.axis_index("expert").astype(jnp.int32).reshape(1)
    half = (lax.axis_index("dp").astype(jnp.int32) & 1).reshape(1)
    routes_t, gates_t = routes.T, route_gates.T

    def sds(shape, dtype=BF):
        return jax.ShapeDtypeStruct(shape, dtype)

    part = sds((cp, width))
    packed = call(
        functools.partial(pack_kernel, peers),
        "pack",
        [part] * (2 * peers) + [sds((rows, count))],
        (me, routes_t, gates_t, tokens, cotangent),
        flops=4 * rows * count * width,
    )
    xs, cs, place = packed[:peers], packed[peers : 2 * peers], packed[2 * peers]
    xs = [xs[0]] + [swap(xs[j], "expert", j) for j in range(1, peers)]
    cs = [cs[0]] + [swap(cs[j], "expert", j) for j in range(1, peers)]
    work = 2 * rows * width * ff
    keep, send = call(
        functools.partial(up_kernel, peers),
        "up",
        [sds((rows // 2, 2 * ff))] * 2,
        (half, *xs, gate_w, up_w),
        flops=2 * work,
    )
    sum_mine, sum_other = reduced(keep, send, dp_count)
    keep, send = call(
        functools.partial(back_kernel, peers),
        "back",
        [sds((rows // 2, ff))] * 2,
        (half, *cs, down_w),
        flops=work,
    )
    dh_mine, dh_other = reduced(keep, send, dp_count)
    *outs, hidden, sums = call(
        functools.partial(out_kernel, peers),
        "out",
        [part] * peers + [sds((rows, ff)), sds((2, rows // 2, 2 * ff))],
        (half, sum_mine, sum_other, down_w),
        flops=work,
    )
    outs = [outs[0]] + [swap(outs[j], "expert", j) for j in range(1, peers)]
    *dxs, dgate, dup = call(
        functools.partial(dx_kernel, peers, cap),
        "dx",
        [part] * peers + [sds((rows, ff))] * 2,
        (half, sums, hidden, dh_mine, dh_other, gate_w, up_w),
        scratch=[pltpu.VMEM((2, rows // 2, ff), BF), pltpu.VMEM((rows, 1), F32)],
        flops=2 * work,
    )
    dxs = [dxs[0]] + [swap(dxs[j], "expert", j) for j in range(1, peers)]
    grad_gate, grad_up, grad_down = call(
        functools.partial(grad_kernel, peers),
        "grads",
        [sds((width, ff))] * 2 + [sds((ff, width))],
        (*xs, *cs, hidden, dgate, dup),
        scalars=0,
        flops=3 * work,
    )
    mixed, grad_tokens, gates_grad = call(
        functools.partial(merge_kernel, peers, cap),
        "merge",
        [sds((count, width))] * 2 + [sds((top, count), F32)],
        (me, routes_t, gates_t, place, *outs, *dxs),
        flops=6 * rows * count * width,
    )
    return (mixed, grad_tokens, gates_grad.T, grad_gate[None], grad_up[None], grad_down[None])


def solution(mesh):
    in_specs = (
        P(("group", "expert"), "dp"),
        P(("group", "expert"), "dp"),
        P(("group", "expert"), None),
        P(("group", "expert"), None),
        P("expert", "dp", None),
        P("expert", "dp", None),
        P("expert", None, "dp"),
    )
    out_specs = (
        P(("group", "expert"), "dp"),
        P(("group", "expert"), "dp"),
        P(("group", "expert"), None),
        P(("group", "expert"), "dp", None),
        P(("group", "expert"), "dp", None),
        P(("group", "expert"), None, "dp"),
    )
    return jax.shard_map(shards, mesh=mesh, in_specs=in_specs, out_specs=out_specs, check_vma=False)
```

```python
import functools

import jax
import jax.numpy as jnp
from jax import lax
from jax.experimental import pallas as pl
from jax.experimental.pallas import tpu as pltpu
from jax.sharding import PartitionSpec as P

BF = jnp.bfloat16
F32 = jnp.float32
VMEM_BYTES = 40 * 1024 * 1024
SYNC = (True, False, False, False)


def swap(block, axis, offset):
    count = lax.axis_size(axis)
    return lax.ppermute(block, axis, [(i, i ^ offset) for i in range(count)])


def dot(a, b):
    return lax.dot_general(a, b, (((1,), (0,)), ((), ())), preferred_element_type=F32)


def dot_nt(a, b):
    return lax.dot_general(a, b, (((1,), (1,)), ((), ())), preferred_element_type=F32)


def dot_tn(a, b):
    return lax.dot_general(a, b, (((0,), (0,)), ((), ())), preferred_element_type=F32)


def call(kernel, name, outs, args, scalars=1, hbm=0, scratch=(), flops=0):
    smem = pl.BlockSpec(memory_space=pltpu.SMEM)
    vmem = pl.BlockSpec(memory_space=pltpu.VMEM)
    moved = sum(a.size * a.dtype.itemsize for a in args) + sum(
        o.size * o.dtype.itemsize for o in outs
    )
    return pl.pallas_call(
        kernel,
        name=name,
        out_shape=outs,
        in_specs=[smem] * scalars
        + [pl.BlockSpec(memory_space=pltpu.HBM)] * hbm
        + [vmem] * (len(args) - scalars - hbm),
        out_specs=[vmem] * len(outs),
        scratch_shapes=list(scratch),
        compiler_params=pltpu.CompilerParams(vmem_limit_bytes=VMEM_BYTES),
        cost_estimate=pl.CostEstimate(flops=flops, bytes_accessed=moved, transcendentals=0),
    )(*args)


def chosen(routes, expert):
    return jnp.sum((routes == expert).astype(F32), axis=0, keepdims=True)


def gate_row(routes, gates, expert):
    return jnp.sum(jnp.where(routes == expert, gates, 0.0), axis=0, keepdims=True)


def pack_kernel(peers, me_ref, routes_ref, tokens_ref, *refs):
    near = peers // 2
    near_ref, x_refs, place_ref = refs[0], refs[1 : 1 + near], refs[1 + near]
    me = me_ref[0]
    count = routes_ref.shape[1]
    rows = x_refs[0].shape[0]
    earlier = (
        lax.broadcasted_iota(jnp.int32, (count, count), 0)
        < lax.broadcasted_iota(jnp.int32, (count, count), 1)
    ).astype(BF)
    slot = lax.broadcasted_iota(jnp.int32, (rows, count), 0)
    routes = routes_ref[...]
    taken = jnp.concatenate([chosen(routes, me ^ j) for j in range(peers)], axis=0)
    rank = dot(taken.astype(BF), earlier)
    rank = jnp.where(taken > 0.0, rank, -1.0).astype(jnp.int32)
    for j in range(peers):
        part = slice(j * rows, (j + 1) * rows)
        place_ref[part, :] = (slot == rank[j : j + 1]).astype(F32).astype(BF)
    tokens = tokens_ref[...]
    for j in range(near):
        part = slice((near + j) * rows, (near + j + 1) * rows)
        x_refs[j][...] = dot(place_ref[part, :], tokens).astype(BF)
    near_ref[...] = dot(place_ref[: near * rows, :], tokens).astype(BF)


def pack_cot_kernel(peers, me_ref, routes_ref, gates_ref, cot_ref, x_ref, place_ref, *refs):
    near = peers // 2
    pair_refs, c_refs = refs[:near], refs[near:]
    me = me_ref[0]
    rows = c_refs[0].shape[0]
    routes, gates = routes_ref[...], gates_ref[...]
    cot = cot_ref[...]
    for j in reversed(range(peers)):
        place = place_ref[j * rows : (j + 1) * rows, :]
        gate = gate_row(routes, gates, me ^ j)
        scale = jnp.sum(place.astype(F32) * gate, axis=1, keepdims=True)
        c = (dot(place, cot) * scale).astype(BF)
        if j < near:
            pair_refs[j][:rows, :] = x_ref[j * rows : (j + 1) * rows, :]
            pair_refs[j][rows:, :] = c
        else:
            c_refs[j - near][...] = c


def load_kernel(*refs):
    count = (len(refs) - 1) // 2
    sem = refs[-1]
    copies = [pltpu.make_async_copy(refs[i], refs[count + i], sem.at[i]) for i in range(count)]
    for copy in copies:
        copy.start()
    for copy in copies:
        copy.wait()


def hand_out(half, y, refs):
    rows = y.shape[0] // 2
    width = y.shape[1]
    lanes = pl.ds(half[1], width)
    if len(refs) == 1:
        refs[0][0, :, lanes] = y[:rows]
        refs[0][1, :, lanes] = y[rows:]
        return
    for h in range(2):

        @pl.when(half[0] == h)
        def _():
            refs[0][:, lanes] = y[h * rows : (h + 1) * rows]
            refs[1][:, lanes] = y[(1 - h) * rows : (2 - h) * rows]


def both_halves(half, refs, store_ref):
    if len(refs) == 1:
        return refs[0]
    store_ref[half] = refs[0][...]
    store_ref[1 - half] = refs[1][...]
    return store_ref


def stack(refs, part=slice(None)):
    return jnp.concatenate([r[part, :] for r in refs], axis=0)


def rows_of(pair_refs, refs, which):
    cp = refs[0].shape[0]
    return jnp.concatenate(
        [stack(pair_refs, slice(which * cp, (which + 1) * cp)), stack(refs)], axis=0
    )


def up_kernel(near, half_ref, *refs):
    pair_refs, x_refs, (gate_ref, up_ref, *to_refs) = refs[:near], refs[near : 2 * near], refs[2 * near :]
    x = rows_of(pair_refs, x_refs, 0)
    width = gate_ref.shape[1]
    hand_out((half_ref[0], 0), dot(x, gate_ref[...]).astype(BF), to_refs)
    hand_out((half_ref[0], width), dot(x, up_ref[...]).astype(BF), to_refs)


def back_kernel(near, half_ref, *refs):
    pair_refs, c_refs, (down_ref, *to_refs) = refs[:near], refs[near : 2 * near], refs[2 * near :]
    c = rows_of(pair_refs, c_refs, 1)
    hand_out((half_ref[0], 0), dot_nt(c, down_ref[...]).astype(BF), to_refs)


def activate(g, u):
    return (g * jax.nn.sigmoid(g) * u).astype(BF)


def derive(g, u, dh):
    s = jax.nn.sigmoid(g)
    return (dh * u * s * (1.0 + g * (1.0 - s))).astype(BF), (dh * (g * s)).astype(BF)


def row_dots(hidden, dh):
    return jnp.sum(hidden.astype(F32) * dh, axis=1, keepdims=True)


def store_dx(cap, dx_ref, block, dots):
    cp = dx_ref.shape[0]
    lanes = 128 * (-(-cp // 128))
    row = lax.broadcasted_iota(jnp.int32, (cp, lanes), 0)
    eye = row == lax.broadcasted_iota(jnp.int32, (cp, lanes), 1)
    dots = jnp.sum(jnp.where(eye, dots, 0.0), axis=0, keepdims=True)
    high = dots.astype(BF).astype(F32)
    middle = (dots - high).astype(BF).astype(F32)
    low = dots - high - middle
    first = jnp.where(row == cap, high, block[:, :lanes])
    first = jnp.where(row == cap + 1, middle, first)
    first = jnp.where(row == cap + 2, low, first)
    dx_ref[:, :lanes] = first.astype(BF)
    dx_ref[:, lanes:] = block[:, lanes:].astype(BF)


def out_kernel(peers, waits, half_ref, down_ref, *refs):
    from_refs, refs = refs[: 2 - waits], refs[2 - waits :]
    out_refs, hidden_ref, sums_ref = refs[:peers], refs[peers], refs[-1]
    width = down_ref.shape[0]
    source_ref = both_halves(half_ref[0], from_refs, sums_ref)
    rows = source_ref.shape[1]
    for h in range(2):
        g = source_ref[h, :, :width].astype(F32)
        u = source_ref[h, :, width:].astype(F32)
        hidden_ref[h * rows : (h + 1) * rows, :] = activate(g, u)
    out = dot(hidden_ref[...], down_ref[...]).astype(BF)
    cp = out_refs[0].shape[0]
    for j in range(peers):
        out_refs[j][...] = out[j * cp : (j + 1) * cp]


def dx_kernel(peers, cap, half_ref, sums_ref, hidden_ref, gate_ref, up_ref, *refs):
    from_refs = refs[: -peers - 4]
    dx_refs, (dgate_ref, dup_ref, dh_ref, dot_ref) = refs[-peers - 4 : -4], refs[-4:]
    width = gate_ref.shape[1]
    source_ref = both_halves(half_ref[0], from_refs, dh_ref)
    rows = source_ref.shape[1]
    for h in range(2):
        part = slice(h * rows, (h + 1) * rows)
        g = sums_ref[h, :, :width].astype(F32)
        u = sums_ref[h, :, width:].astype(F32)
        dh = source_ref[h].astype(F32)
        dgate_ref[part, :], dup_ref[part, :] = derive(g, u, dh)
        dot_ref[part, :] = row_dots(hidden_ref[part, :], dh)
    dx = dot_nt(dgate_ref[...], gate_ref[...]) + dot_nt(dup_ref[...], up_ref[...])
    cp = dx_refs[0].shape[0]
    for j in range(peers):
        part = slice(j * cp, (j + 1) * cp)
        store_dx(cap, dx_refs[j], dx[part], dot_ref[part, :])


def grad_kernel(near, *refs):
    pair_refs, x_refs, c_refs = refs[:near], refs[near : 2 * near], refs[2 * near : 3 * near]
    hidden_ref, dgate_ref, dup_ref, gg_ref, gu_ref, gd_ref = refs[3 * near :]
    x = rows_of(pair_refs, x_refs, 0)
    gg_ref[...] = dot_tn(x, dgate_ref[...]).astype(BF)
    gu_ref[...] = dot_tn(x, dup_ref[...]).astype(BF)
    gd_ref[...] = dot_tn(hidden_ref[...], rows_of(pair_refs, c_refs, 1)).astype(BF)


def mix_kernel(peers, me_ref, routes_ref, gates_ref, place_ref, *refs):
    out_refs, mixed_ref = refs[:peers], refs[peers]
    me = me_ref[0]
    routes, gates = routes_ref[...], gates_ref[...]
    cp = out_refs[0].shape[0]
    highs, lows = [], []
    for j in range(peers):
        place = place_ref[j * cp : (j + 1) * cp, :].astype(F32)
        gate = gate_row(routes, gates, me ^ j)
        high = gate.astype(BF).astype(F32)
        highs.append((place * high).astype(BF))
        lows.append((place * (gate - high)).astype(BF))
    out = stack(out_refs)
    mixed = dot_tn(jnp.concatenate(highs, axis=0), out) + dot_tn(jnp.concatenate(lows, axis=0), out)
    mixed_ref[...] = mixed.astype(BF)


def merge_kernel(peers, cap, me_ref, routes_ref, gates_ref, place_ref, *refs):
    dx_refs, (grad_ref, gates_out_ref) = refs[:peers], refs[peers:]
    me = me_ref[0]
    routes, gates = routes_ref[...], gates_ref[...]
    cp = dx_refs[0].shape[0]
    grad_ref[...] = dot_tn(place_ref[...], stack(dx_refs)).astype(BF)
    total = jnp.zeros(gates.shape, F32)
    base = cap // 16 * 16
    at = cap - base
    for j in range(peers):
        place = place_ref[j * cp : (j + 1) * cp, :]
        found = dot(dx_refs[j][base:cp, :cp], place)
        value = found[at : at + 1] + found[at + 1 : at + 2] + found[at + 2 : at + 3]
        total = total + jnp.where(routes == (me ^ j), value, 0.0)
    gates_out_ref[...] = total / gates


def added(a, b):
    return (a.astype(F32) + b.astype(F32)).astype(BF)


def after(first, arrays):
    return lax.optimization_barrier((*first, *arrays))[len(first) :]


def pairs_of(count):
    return [[i, i + 1] for i in range(0, count, 2)]


def reduced(parts, dp_count):
    if len(parts) == 1:
        arrived = lax.all_to_all(parts[0], "dp", 0, 0, axis_index_groups=pairs_of(dp_count))
        total = added(arrived[0], arrived[1])
    else:
        total = added(parts[0], swap(parts[1], "dp", 1))
    bit = 2
    while bit < dp_count:
        total = added(total, swap(total, "dp", bit))
        bit *= 2
    return total


def whole(total, dp_count, waits):
    if waits:
        twice = jnp.broadcast_to(total[None], (2, *total.shape))
        return [lax.all_to_all(twice, "dp", 0, 0, axis_index_groups=pairs_of(dp_count))]
    return [total, swap(total, "dp", 1)]


def shards(tokens, cotangent, routes, route_gates, gate_weight, up_weight, down_weight):
    peers = lax.axis_size("expert")
    near = peers // 2
    dp_count = lax.axis_size("dp")
    count, top = routes.shape
    width = tokens.shape[1]
    ff = gate_weight.shape[2]
    cap = 7 * count * top // (6 * peers)
    cp = -(-(cap + 3) // 16) * 16
    rows = near * cp
    gate_w, up_w, down_w = gate_weight[0], up_weight[0], down_weight[0]
    me = lax.axis_index("expert").astype(jnp.int32).reshape(1)
    half = (lax.axis_index("dp").astype(jnp.int32) & 1).reshape(1)
    routes_t, gates_t = routes.T, route_gates.T

    def sds(shape, dtype=BF):
        return jax.ShapeDtypeStruct(shape, dtype)

    part, pair = sds((cp, width)), sds((2 * cp, width))
    near_x, *xs, place = call(
        functools.partial(pack_kernel, peers),
        "pack",
        [sds((rows, width))] + [part] * near + [sds((2 * rows, count))],
        (me, routes_t, tokens),
        flops=4 * rows * count * width,
    )
    packed = call(
        functools.partial(pack_cot_kernel, peers),
        "pack_cot",
        [pair] * near + [part] * near,
        (me, routes_t, gates_t, cotangent, near_x, place),
        flops=4 * rows * count * width,
    )
    xcs, cs = packed[:near], packed[near:]
    weights = lax.optimization_barrier((gate_w, up_w, down_w, cs[0]))[:3]
    gate_w, up_w, down_w = call(
        load_kernel,
        "load",
        [sds(w.shape) for w in weights],
        weights,
        scalars=0,
        scratch=[pltpu.SemaphoreType.DMA((3,))],
    )
    xs = [swap(xs[j], "expert", near + j) for j in range(near)]
    xcs = [xcs[0]] + [swap(xcs[j], "expert", j) for j in range(1, near)]
    cs = [swap(cs[j], "expert", near + j) for j in range(near)]
    work = 2 * rows * width * ff

    def parts_of(waits, wide):
        return [sds((2, rows, wide))] if waits else [sds((rows, wide))] * 2

    up_parts = call(
        functools.partial(up_kernel, near),
        "up",
        parts_of(SYNC[0], 2 * ff),
        (half, *xcs, *xs, gate_w, up_w),
        flops=4 * work,
    )
    up_sum = reduced(up_parts, dp_count)
    dh_parts = call(
        functools.partial(back_kernel, near),
        "back",
        parts_of(SYNC[1], ff),
        (half, *xcs, *cs, down_w),
        flops=2 * work,
    )
    dh_sum = reduced(dh_parts, dp_count)
    up_both = whole(up_sum, dp_count, SYNC[2])
    produced = call(
        functools.partial(out_kernel, peers, SYNC[2]),
        "out",
        [part] * peers + [sds((2 * rows, ff))] + [sds((2, rows, 2 * ff))] * (not SYNC[2]),
        (half, down_w, *up_both),
        flops=2 * work,
    )
    outs, hidden = produced[:peers], produced[peers]
    sums = up_both[0] if SYNC[2] else produced[-1]
    *dxs, dgate, dup = call(
        functools.partial(dx_kernel, peers, cap),
        "dx",
        [part] * peers + [sds((2 * rows, ff))] * 2,
        (half, sums, hidden, gate_w, up_w, *whole(dh_sum, dp_count, SYNC[3])),
        scratch=[pltpu.VMEM((2, rows, ff), BF), pltpu.VMEM((2 * rows, 1), F32)],
        flops=4 * work,
    )
    outs = [outs[0]] + [swap(outs[j], "expert", j) for j in range(1, peers)]
    dxs = [dxs[0]] + [swap(dxs[j], "expert", j) for j in range(1, peers)]
    grad_gate, grad_up, grad_down = call(
        functools.partial(grad_kernel, near),
        "grads",
        [sds((width, ff))] * 2 + [sds((ff, width))],
        (*xcs, *xs, *cs, hidden, dgate, dup),
        scalars=0,
        flops=6 * work,
    )
    (mixed,) = call(
        functools.partial(mix_kernel, peers),
        "mix",
        [sds((count, width))],
        (me, routes_t, gates_t, place, *outs),
        flops=8 * rows * count * width,
    )
    grad_tokens, gates_grad = call(
        functools.partial(merge_kernel, peers, cap),
        "merge",
        [sds((count, width)), sds((top, count), F32)],
        (me, routes_t, gates_t, place, *dxs),
        flops=4 * rows * count * width,
    )
    return (mixed, grad_tokens, gates_grad.T, grad_gate[None], grad_up[None], grad_down[None])


def solution(mesh):
    in_specs = (
        P(("group", "expert"), "dp"),
        P(("group", "expert"), "dp"),
        P(("group", "expert"), None),
        P(("group", "expert"), None),
        P("expert", "dp", None),
        P("expert", "dp", None),
        P("expert", None, "dp"),
    )
    out_specs = (
        P(("group", "expert"), "dp"),
        P(("group", "expert"), "dp"),
        P(("group", "expert"), None),
        P(("group", "expert"), "dp", None),
        P(("group", "expert"), "dp", None),
        P(("group", "expert"), None, "dp"),
    )
    return jax.shard_map(shards, mesh=mesh, in_specs=in_specs, out_specs=out_specs, check_vma=False)
```

```python
import functools

import jax
import jax.numpy as jnp
from jax import lax
from jax.experimental import pallas as pl
from jax.experimental.pallas import tpu as pltpu
from jax.sharding import PartitionSpec as P

BF = jnp.bfloat16
F32 = jnp.float32
VMEM_BYTES = 40 * 1024 * 1024
DH_AFTER = True
SYNC = (False, False, False, True)


def swap(block, axis, offset):
    count = lax.axis_size(axis)
    return lax.ppermute(block, axis, [(i, i ^ offset) for i in range(count)])


def dot(a, b):
    return lax.dot_general(a, b, (((1,), (0,)), ((), ())), preferred_element_type=F32)


def dot_nt(a, b):
    return lax.dot_general(a, b, (((1,), (1,)), ((), ())), preferred_element_type=F32)


def dot_tn(a, b):
    return lax.dot_general(a, b, (((0,), (0,)), ((), ())), preferred_element_type=F32)


def call(kernel, name, outs, args, scalars=1, hbm=0, scratch=(), flops=0):
    smem = pl.BlockSpec(memory_space=pltpu.SMEM)
    vmem = pl.BlockSpec(memory_space=pltpu.VMEM)
    moved = sum(a.size * a.dtype.itemsize for a in args) + sum(
        o.size * o.dtype.itemsize for o in outs
    )
    return pl.pallas_call(
        kernel,
        name=name,
        out_shape=outs,
        in_specs=[smem] * scalars
        + [pl.BlockSpec(memory_space=pltpu.HBM)] * hbm
        + [vmem] * (len(args) - scalars - hbm),
        out_specs=[vmem] * len(outs),
        scratch_shapes=list(scratch),
        compiler_params=pltpu.CompilerParams(vmem_limit_bytes=VMEM_BYTES),
        cost_estimate=pl.CostEstimate(flops=flops, bytes_accessed=moved, transcendentals=0),
    )(*args)


def chosen(routes, expert):
    return jnp.sum((routes == expert).astype(F32), axis=0, keepdims=True)


def gate_row(routes, gates, expert):
    return jnp.sum(jnp.where(routes == expert, gates, 0.0), axis=0, keepdims=True)


def pack_kernel(peers, me_ref, routes_ref, tokens_ref, *refs):
    x_refs, place_ref = refs[:peers], refs[peers]
    me = me_ref[0]
    count = routes_ref.shape[1]
    rows = x_refs[0].shape[0]
    earlier = (
        lax.broadcasted_iota(jnp.int32, (count, count), 0)
        < lax.broadcasted_iota(jnp.int32, (count, count), 1)
    ).astype(BF)
    slot = lax.broadcasted_iota(jnp.int32, (rows, count), 0)
    routes = routes_ref[...]
    taken = jnp.concatenate([chosen(routes, me ^ j) for j in range(peers)], axis=0)
    rank = dot(taken.astype(BF), earlier)
    rank = jnp.where(taken > 0.0, rank, -1.0).astype(jnp.int32)
    for j in range(peers):
        part = slice(j * rows, (j + 1) * rows)
        place_ref[part, :] = (slot == rank[j : j + 1]).astype(F32).astype(BF)
    tokens = tokens_ref[...]
    for j in reversed(range(peers)):
        part = slice(j * rows, (j + 1) * rows)
        x_refs[j][...] = dot(place_ref[part, :], tokens).astype(BF)


def pack_cot_kernel(peers, me_ref, routes_ref, gates_ref, cot_ref, place_ref, *c_refs):
    me = me_ref[0]
    rows = c_refs[0].shape[0]
    routes, gates = routes_ref[...], gates_ref[...]
    cot = cot_ref[...]
    for j in reversed(range(peers)):
        place = place_ref[j * rows : (j + 1) * rows, :]
        gate = gate_row(routes, gates, me ^ j)
        scale = jnp.sum(place.astype(F32) * gate, axis=1, keepdims=True)
        c_refs[j][...] = (dot(place, cot) * scale).astype(BF)


def load_kernel(*refs):
    count = (len(refs) - 1) // 2
    sem = refs[-1]
    copies = [pltpu.make_async_copy(refs[i], refs[count + i], sem.at[i]) for i in range(count)]
    for copy in copies:
        copy.start()
    for copy in copies:
        copy.wait()


def hand_out(half, y, refs):
    rows = y.shape[0] // 2
    width = y.shape[1]
    lanes = pl.ds(half[1], width)
    if len(refs) == 1:
        refs[0][0, :, lanes] = y[:rows]
        refs[0][1, :, lanes] = y[rows:]
        return
    for h in range(2):

        @pl.when(half[0] == h)
        def _():
            refs[0][:, lanes] = y[h * rows : (h + 1) * rows]
            refs[1][:, lanes] = y[(1 - h) * rows : (2 - h) * rows]


def both_halves(half, refs, store_ref):
    if len(refs) == 1:
        return refs[0]
    store_ref[half] = refs[0][...]
    store_ref[1 - half] = refs[1][...]
    return store_ref


def stack(refs, part=slice(None)):
    return jnp.concatenate([r[part, :] for r in refs], axis=0)


def up_kernel(peers, half_ref, *refs):
    x_refs, (gate_ref, up_ref, *to_refs) = refs[:peers], refs[peers:]
    x = stack(x_refs)
    width = gate_ref.shape[1]
    hand_out((half_ref[0], 0), dot(x, gate_ref[...]).astype(BF), to_refs)
    hand_out((half_ref[0], width), dot(x, up_ref[...]).astype(BF), to_refs)


def back_kernel(peers, half_ref, *refs):
    c_refs, (down_ref, *to_refs) = refs[:peers], refs[peers:]
    hand_out((half_ref[0], 0), dot_nt(stack(c_refs), down_ref[...]).astype(BF), to_refs)


def activate(g, u):
    return (g * jax.nn.sigmoid(g) * u).astype(BF)


def derive(g, u, dh):
    s = jax.nn.sigmoid(g)
    return (dh * u * s * (1.0 + g * (1.0 - s))).astype(BF), (dh * (g * s)).astype(BF)


def row_dots(hidden, dh):
    return jnp.sum(hidden.astype(F32) * dh, axis=1, keepdims=True)


def store_dx(cap, dx_ref, block, dots):
    cp = dx_ref.shape[0]
    lanes = 128 * (-(-cp // 128))
    row = lax.broadcasted_iota(jnp.int32, (cp, lanes), 0)
    eye = row == lax.broadcasted_iota(jnp.int32, (cp, lanes), 1)
    dots = jnp.sum(jnp.where(eye, dots, 0.0), axis=0, keepdims=True)
    high = dots.astype(BF).astype(F32)
    middle = (dots - high).astype(BF).astype(F32)
    low = dots - high - middle
    first = jnp.where(row == cap, high, block[:, :lanes])
    first = jnp.where(row == cap + 1, middle, first)
    first = jnp.where(row == cap + 2, low, first)
    dx_ref[:, :lanes] = first.astype(BF)
    dx_ref[:, lanes:] = block[:, lanes:].astype(BF)


def out_kernel(peers, waits, half_ref, down_ref, *refs):
    from_refs, refs = refs[: 2 - waits], refs[2 - waits :]
    out_refs, hidden_ref, sums_ref = refs[:peers], refs[peers], refs[-1]
    width = down_ref.shape[0]
    source_ref = both_halves(half_ref[0], from_refs, sums_ref)
    rows = source_ref.shape[1]
    for h in range(2):
        g = source_ref[h, :, :width].astype(F32)
        u = source_ref[h, :, width:].astype(F32)
        hidden_ref[h * rows : (h + 1) * rows, :] = activate(g, u)
    out = dot(hidden_ref[...], down_ref[...]).astype(BF)
    cp = out_refs[0].shape[0]
    for j in range(peers):
        out_refs[j][...] = out[j * cp : (j + 1) * cp]


def dx_kernel(peers, cap, half_ref, sums_ref, hidden_ref, gate_ref, up_ref, *refs):
    from_refs = refs[: -peers - 4]
    dx_refs, (dgate_ref, dup_ref, dh_ref, dot_ref) = refs[-peers - 4 : -4], refs[-4:]
    width = gate_ref.shape[1]
    source_ref = both_halves(half_ref[0], from_refs, dh_ref)
    rows = source_ref.shape[1]
    for h in range(2):
        part = slice(h * rows, (h + 1) * rows)
        g = sums_ref[h, :, :width].astype(F32)
        u = sums_ref[h, :, width:].astype(F32)
        dh = source_ref[h].astype(F32)
        dgate_ref[part, :], dup_ref[part, :] = derive(g, u, dh)
        dot_ref[part, :] = row_dots(hidden_ref[part, :], dh)
    dx = dot_nt(dgate_ref[...], gate_ref[...]) + dot_nt(dup_ref[...], up_ref[...])
    cp = dx_refs[0].shape[0]
    for j in range(peers):
        part = slice(j * cp, (j + 1) * cp)
        store_dx(cap, dx_refs[j], dx[part], dot_ref[part, :])


def grad_kernel(peers, *refs):
    x_refs, c_refs = refs[:peers], refs[peers : 2 * peers]
    hidden_ref, dgate_ref, dup_ref, gg_ref, gu_ref, gd_ref = refs[2 * peers :]
    x = stack(x_refs)
    gg_ref[...] = dot_tn(x, dgate_ref[...]).astype(BF)
    gu_ref[...] = dot_tn(x, dup_ref[...]).astype(BF)
    gd_ref[...] = dot_tn(hidden_ref[...], stack(c_refs)).astype(BF)


def mix_kernel(peers, me_ref, routes_ref, gates_ref, place_ref, *refs):
    out_refs, mixed_ref = refs[:peers], refs[peers]
    me = me_ref[0]
    routes, gates = routes_ref[...], gates_ref[...]
    cp = out_refs[0].shape[0]
    highs, lows = [], []
    for j in range(peers):
        place = place_ref[j * cp : (j + 1) * cp, :].astype(F32)
        gate = gate_row(routes, gates, me ^ j)
        high = gate.astype(BF).astype(F32)
        highs.append((place * high).astype(BF))
        lows.append((place * (gate - high)).astype(BF))
    out = stack(out_refs)
    mixed = dot_tn(jnp.concatenate(highs, axis=0), out) + dot_tn(jnp.concatenate(lows, axis=0), out)
    mixed_ref[...] = mixed.astype(BF)


def merge_kernel(peers, cap, me_ref, routes_ref, gates_ref, place_ref, *refs):
    dx_refs, (grad_ref, gates_out_ref) = refs[:peers], refs[peers:]
    me = me_ref[0]
    routes, gates = routes_ref[...], gates_ref[...]
    cp = dx_refs[0].shape[0]
    grad_ref[...] = dot_tn(place_ref[...], stack(dx_refs)).astype(BF)
    total = jnp.zeros(gates.shape, F32)
    base = cap // 16 * 16
    at = cap - base
    for j in range(peers):
        place = place_ref[j * cp : (j + 1) * cp, :]
        found = dot(dx_refs[j][base:cp, :cp], place)
        value = found[at : at + 1] + found[at + 1 : at + 2] + found[at + 2 : at + 3]
        total = total + jnp.where(routes == (me ^ j), value, 0.0)
    gates_out_ref[...] = total / gates


def added(a, b):
    return (a.astype(F32) + b.astype(F32)).astype(BF)


def after(first, arrays):
    return lax.optimization_barrier((*first, *arrays))[len(first) :]


def pairs_of(count):
    return [[i, i + 1] for i in range(0, count, 2)]


def reduced(parts, dp_count, first=()):
    if len(parts) == 1:
        arrived = lax.all_to_all(parts[0], "dp", 0, 0, axis_index_groups=pairs_of(dp_count))
        total = added(arrived[0], arrived[1])
    else:
        total = added(parts[0], swap(parts[1], "dp", 1))
    bit = 2
    while bit < dp_count:
        arrived = swap(total, "dp", bit)
        bit *= 2
        if first and bit >= dp_count:
            (arrived,) = after(first, (arrived,))
        total = added(total, arrived)
    return total


def whole(total, dp_count, waits):
    if waits:
        twice = jnp.broadcast_to(total[None], (2, *total.shape))
        return [lax.all_to_all(twice, "dp", 0, 0, axis_index_groups=pairs_of(dp_count))]
    return [total, swap(total, "dp", 1)]


def shards(tokens, cotangent, routes, route_gates, gate_weight, up_weight, down_weight):
    peers = lax.axis_size("expert")
    near = peers // 2
    dp_count = lax.axis_size("dp")
    count, top = routes.shape
    width = tokens.shape[1]
    ff = gate_weight.shape[2]
    cap = 7 * count * top // (6 * peers)
    cp = -(-(cap + 3) // 16) * 16
    rows = near * cp
    gate_w, up_w, down_w = gate_weight[0], up_weight[0], down_weight[0]
    me = lax.axis_index("expert").astype(jnp.int32).reshape(1)
    half = (lax.axis_index("dp").astype(jnp.int32) & 1).reshape(1)
    routes_t, gates_t = routes.T, route_gates.T

    def sds(shape, dtype=BF):
        return jax.ShapeDtypeStruct(shape, dtype)

    part = sds((cp, width))
    *xs, place = call(
        functools.partial(pack_kernel, peers),
        "pack",
        [part] * peers + [sds((2 * rows, count))],
        (me, routes_t, tokens),
        flops=4 * rows * count * width,
    )
    cs = call(
        functools.partial(pack_cot_kernel, peers),
        "pack_cot",
        [part] * peers,
        (me, routes_t, gates_t, cotangent, place),
        flops=4 * rows * count * width,
    )
    weights = lax.optimization_barrier((gate_w, up_w, down_w, cs[0]))[:3]
    gate_w, up_w, down_w = call(
        load_kernel,
        "load",
        [sds(w.shape) for w in weights],
        weights,
        scalars=0,
        scratch=[pltpu.SemaphoreType.DMA((3,))],
    )
    xs = [xs[0]] + [swap(xs[j], "expert", j) for j in range(1, peers)]
    cs = [cs[0]] + [swap(cs[j], "expert", j) for j in range(1, peers)]
    work = 2 * rows * width * ff

    def parts_of(waits, wide):
        return [sds((2, rows, wide))] if waits else [sds((rows, wide))] * 2

    up_parts = call(
        functools.partial(up_kernel, peers),
        "up",
        parts_of(SYNC[0], 2 * ff),
        (half, *xs, gate_w, up_w),
        flops=4 * work,
    )
    up_sum = reduced(up_parts, dp_count)
    dh_parts = call(
        functools.partial(back_kernel, peers),
        "back",
        parts_of(SYNC[1], ff),
        (half, *cs, down_w),
        flops=2 * work,
    )
    up_both = whole(up_sum, dp_count, SYNC[2])
    produced = call(
        functools.partial(out_kernel, peers, SYNC[2]),
        "out",
        [part] * peers + [sds((2 * rows, ff))] + [sds((2, rows, 2 * ff))] * (not SYNC[2]),
        (half, down_w, *up_both),
        flops=2 * work,
    )
    outs, hidden = produced[:peers], produced[peers]
    sums = up_both[0] if SYNC[2] else produced[-1]
    dh_sum = reduced(dh_parts, dp_count, DH_AFTER and (outs[0],))
    *dxs, dgate, dup = call(
        functools.partial(dx_kernel, peers, cap),
        "dx",
        [part] * peers + [sds((2 * rows, ff))] * 2,
        (half, sums, hidden, gate_w, up_w, *whole(dh_sum, dp_count, SYNC[3])),
        scratch=[pltpu.VMEM((2, rows, ff), BF), pltpu.VMEM((2 * rows, 1), F32)],
        flops=4 * work,
    )
    outs = [outs[0]] + [swap(outs[j], "expert", j) for j in range(1, peers)]
    dxs = [dxs[0]] + [swap(dxs[j], "expert", j) for j in range(1, peers)]
    grad_gate, grad_up, grad_down = call(
        functools.partial(grad_kernel, peers),
        "grads",
        [sds((width, ff))] * 2 + [sds((ff, width))],
        (*xs, *cs, hidden, dgate, dup),
        scalars=0,
        flops=6 * work,
    )
    (mixed,) = call(
        functools.partial(mix_kernel, peers),
        "mix",
        [sds((count, width))],
        (me, routes_t, gates_t, place, *outs),
        flops=8 * rows * count * width,
    )
    grad_tokens, gates_grad = call(
        functools.partial(merge_kernel, peers, cap),
        "merge",
        [sds((count, width)), sds((top, count), F32)],
        (me, routes_t, gates_t, place, *dxs),
        flops=4 * rows * count * width,
    )
    return (mixed, grad_tokens, gates_grad.T, grad_gate[None], grad_up[None], grad_down[None])


def solution(mesh):
    in_specs = (
        P(("group", "expert"), "dp"),
        P(("group", "expert"), "dp"),
        P(("group", "expert"), None),
        P(("group", "expert"), None),
        P("expert", "dp", None),
        P("expert", "dp", None),
        P("expert", None, "dp"),
    )
    out_specs = (
        P(("group", "expert"), "dp"),
        P(("group", "expert"), "dp"),
        P(("group", "expert"), None),
        P(("group", "expert"), "dp", None),
        P(("group", "expert"), "dp", None),
        P(("group", "expert"), None, "dp"),
    )
    return jax.shard_map(shards, mesh=mesh, in_specs=in_specs, out_specs=out_specs, check_vma=False)
```

```python
import functools

import jax
import jax.numpy as jnp
from jax import lax
from jax.experimental import pallas as pl
from jax.experimental.pallas import tpu as pltpu
from jax.sharding import PartitionSpec as P

BF = jnp.bfloat16
F32 = jnp.float32
VMEM_BYTES = 40 * 1024 * 1024
NEAR_PIECES, DH_PIECES, DX_FLOPS = 2, 3, 0
NEAR_AFTER, DH_AFTER = True, True


def swap(block, axis, offset):
    count = lax.axis_size(axis)
    return lax.ppermute(block, axis, [(i, i ^ offset) for i in range(count)])


def dot(a, b):
    return lax.dot_general(a, b, (((1,), (0,)), ((), ())), preferred_element_type=F32)


def dot_nt(a, b):
    return lax.dot_general(a, b, (((1,), (1,)), ((), ())), preferred_element_type=F32)


def dot_tn(a, b):
    return lax.dot_general(a, b, (((0,), (0,)), ((), ())), preferred_element_type=F32)


def call(kernel, name, outs, args, scalars=1, hbm=0, scratch=(), flops=0):
    smem = pl.BlockSpec(memory_space=pltpu.SMEM)
    vmem = pl.BlockSpec(memory_space=pltpu.VMEM)
    moved = sum(a.size * a.dtype.itemsize for a in args) + sum(
        o.size * o.dtype.itemsize for o in outs
    )
    return pl.pallas_call(
        kernel,
        name=name,
        out_shape=outs,
        in_specs=[smem] * scalars
        + [pl.BlockSpec(memory_space=pltpu.HBM)] * hbm
        + [vmem] * (len(args) - scalars - hbm),
        out_specs=[vmem] * len(outs),
        scratch_shapes=list(scratch),
        compiler_params=pltpu.CompilerParams(vmem_limit_bytes=VMEM_BYTES),
        cost_estimate=pl.CostEstimate(flops=flops, bytes_accessed=moved, transcendentals=0),
    )(*args)


def chosen(routes, expert):
    return jnp.sum((routes == expert).astype(F32), axis=0, keepdims=True)


def gate_row(routes, gates, expert):
    return jnp.sum(jnp.where(routes == expert, gates, 0.0), axis=0, keepdims=True)


def pack_kernel(peers, me_ref, routes_ref, tokens_ref, *refs):
    x_refs, place_ref = refs[:peers], refs[peers]
    me = me_ref[0]
    count = routes_ref.shape[1]
    rows = x_refs[0].shape[0]
    earlier = (
        lax.broadcasted_iota(jnp.int32, (count, count), 0)
        < lax.broadcasted_iota(jnp.int32, (count, count), 1)
    ).astype(BF)
    slot = lax.broadcasted_iota(jnp.int32, (rows, count), 0)
    routes = routes_ref[...]
    taken = jnp.concatenate([chosen(routes, me ^ j) for j in range(peers)], axis=0)
    rank = dot(taken.astype(BF), earlier)
    rank = jnp.where(taken > 0.0, rank, -1.0).astype(jnp.int32)
    for j in range(peers):
        part = slice(j * rows, (j + 1) * rows)
        place_ref[part, :] = (slot == rank[j : j + 1]).astype(F32).astype(BF)
    tokens = tokens_ref[...]
    for j in reversed(range(peers)):
        part = slice(j * rows, (j + 1) * rows)
        x_refs[j][...] = dot(place_ref[part, :], tokens).astype(BF)


def pack_cot_kernel(peers, me_ref, routes_ref, gates_ref, cot_ref, place_ref, *c_refs):
    me = me_ref[0]
    rows = c_refs[0].shape[0]
    routes, gates = routes_ref[...], gates_ref[...]
    cot = cot_ref[...]
    for j in reversed(range(peers)):
        place = place_ref[j * rows : (j + 1) * rows, :]
        gate = gate_row(routes, gates, me ^ j)
        scale = jnp.sum(place.astype(F32) * gate, axis=1, keepdims=True)
        c_refs[j][...] = (dot(place, cot) * scale).astype(BF)


def load_kernel(*refs):
    count = (len(refs) - 1) // 2
    sem = refs[-1]
    copies = [pltpu.make_async_copy(refs[i], refs[count + i], sem.at[i]) for i in range(count)]
    for copy in copies:
        copy.start()
    for copy in copies:
        copy.wait()


def hand_out(half, y, start, lane, keep_ref, send_ref):
    rows = y.shape[0] // 2
    target = (slice(start, start + rows), slice(lane, lane + y.shape[1]))
    for h in range(2):

        @pl.when(half == h)
        def _():
            keep_ref[target] = y[h * rows : (h + 1) * rows]
            send_ref[target] = y[(1 - h) * rows : (2 - h) * rows]


def stack(refs, part=slice(None)):
    return jnp.concatenate([r[part, :] for r in refs], axis=0)


def up_kernel(near, half_ref, *refs):
    x_refs, (gate_ref, up_ref, near_keep, near_send, far_keep, far_send) = refs[:-6], refs[-6:]
    x_refs = x_refs[near:] + x_refs[:near]
    half = half_ref[0]
    x = stack(x_refs)
    rows = near * x_refs[0].shape[0]
    width = gate_ref.shape[1]
    for i, w_ref in enumerate((gate_ref, up_ref)):
        y = dot(x, w_ref[...]).astype(BF)
        hand_out(half, y[:rows], 0, i * width, near_keep, near_send)
        hand_out(half, y[rows:], 0, i * width, far_keep, far_send)


def back_kernel(near, half_ref, *refs):
    c_refs, (down_ref, keep_ref, send_ref) = refs[:-3], refs[-3:]
    c_refs = c_refs[near:] + c_refs[:near]
    half = half_ref[0]
    y = dot_nt(stack(c_refs), down_ref[...]).astype(BF)
    rows = near * c_refs[0].shape[0]
    hand_out(half, y[:rows], 0, 0, keep_ref, send_ref)
    hand_out(half, y[rows:], rows // 2, 0, keep_ref, send_ref)


def activate(g, u):
    return (g * jax.nn.sigmoid(g) * u).astype(BF)


def derive(g, u, dh):
    s = jax.nn.sigmoid(g)
    return (dh * u * s * (1.0 + g * (1.0 - s))).astype(BF), (dh * (g * s)).astype(BF)


def row_dots(hidden, dh):
    return jnp.sum(hidden.astype(F32) * dh, axis=1, keepdims=True)


def store_dx(cap, dx_ref, block, dots):
    cp = block.shape[0]
    lanes = 128 * (-(-cp // 128))
    row = lax.broadcasted_iota(jnp.int32, (cp, lanes), 0)
    eye = row == lax.broadcasted_iota(jnp.int32, (cp, lanes), 1)
    dots = jnp.sum(jnp.where(eye, dots, 0.0), axis=0, keepdims=True)
    high = dots.astype(BF).astype(F32)
    middle = (dots - high).astype(BF).astype(F32)
    low = dots - high - middle
    first = jnp.where(row == cap, high, block[:, :lanes])
    first = jnp.where(row == cap + 1, middle, first)
    first = jnp.where(row == cap + 2, low, first)
    dx_ref[:, :lanes] = first.astype(BF)
    dx_ref[:, lanes:] = block[:, lanes:].astype(BF)


def out_kernel(near, half_ref, mine_ref, other_ref, down_ref, *refs):
    out_refs, (hidden_ref, sums_ref) = refs[:near], refs[near:]
    half = half_ref[0]
    width = down_ref.shape[0]
    sums_ref[half] = mine_ref[...]
    sums_ref[1 - half] = other_ref[...]
    rows = mine_ref.shape[0]
    for h in range(2):
        g = sums_ref[h, :, :width].astype(F32)
        u = sums_ref[h, :, width:].astype(F32)
        hidden_ref[h * rows : (h + 1) * rows, :] = activate(g, u)
    out = dot(hidden_ref[...], down_ref[...]).astype(BF)
    cp = out_refs[0].shape[0]
    for j in range(near):
        out_refs[j][...] = out[j * cp : (j + 1) * cp]


def gather(half, refs, target_ref):
    count = len(refs) // 2
    wide = refs[0].shape[1]
    for i in range(count):
        target_ref[half, :, i * wide : (i + 1) * wide] = refs[i][...]
        target_ref[1 - half, :, i * wide : (i + 1) * wide] = refs[count + i][...]


def dx_rows(rows, width, source_ref, dh_ref, first, hidden_ref, dgate_ref, dup_ref, dot_ref):
    for h in range(2):
        part = slice(h * rows, (h + 1) * rows)
        g = source_ref[h, :, :width].astype(F32)
        u = source_ref[h, :, width:].astype(F32)
        dh = dh_ref[h, first : first + rows, :].astype(F32)
        dgate_ref[part, :], dup_ref[part, :] = derive(g, u, dh)
        dot_ref[part, :] = row_dots(hidden_ref[part, :], dh)


def dx_kernel(near, cap, half_ref, far_ref, hidden_ref, gate_ref, up_ref, *refs):
    dh_sums, refs = refs[: 2 * DH_PIECES], refs[2 * DH_PIECES :]
    dx_refs, (dgate_ref, dup_ref, dh_ref, dot_ref) = refs[:near], refs[near:]
    gather(half_ref[0], dh_sums, dh_ref)
    rows = far_ref.shape[1]
    dx_rows(rows, gate_ref.shape[1], far_ref, dh_ref, rows, hidden_ref, dgate_ref, dup_ref, dot_ref)
    dx = dot_nt(dgate_ref[...], gate_ref[...]) + dot_nt(dup_ref[...], up_ref[...])
    cp = dx_refs[0].shape[0]
    for j in range(near):
        part = slice(j * cp, (j + 1) * cp)
        store_dx(cap, dx_refs[j], dx[part], dot_ref[part, :])


def near_kernel(near, cap, half_ref, dh_ref, gate_ref, up_ref, down_ref, *refs):
    near_sums, refs = refs[: 2 * NEAR_PIECES], refs[2 * NEAR_PIECES :]
    out_refs, dx_refs, refs = refs[:near], refs[near : 2 * near], refs[2 * near :]
    hidden_ref, dgate_ref, dup_ref, near_ref, dot_ref = refs
    gather(half_ref[0], near_sums, near_ref)
    rows, width = near_ref.shape[1], gate_ref.shape[1]
    for h in range(2):
        g = near_ref[h, :, :width].astype(F32)
        u = near_ref[h, :, width:].astype(F32)
        hidden_ref[h * rows : (h + 1) * rows, :] = activate(g, u)
    dx_rows(rows, width, near_ref, dh_ref, 0, hidden_ref, dgate_ref, dup_ref, dot_ref)
    out = dot(hidden_ref[...], down_ref[...]).astype(BF)
    dx = dot_nt(dgate_ref[...], gate_ref[...]) + dot_nt(dup_ref[...], up_ref[...])
    cp = dx_refs[0].shape[0]
    for j in range(near):
        part = slice(j * cp, (j + 1) * cp)
        out_refs[j][...] = out[part]
        store_dx(cap, dx_refs[j], dx[part], dot_ref[part, :])


def grad_kernel(peers, *refs):
    x_refs, c_refs = refs[:peers], refs[peers : 2 * peers]
    hidden_refs, dgate_refs, dup_refs = (refs[2 * peers + 2 * i :][:2] for i in range(3))
    gg_ref, gu_ref, gd_ref = refs[2 * peers + 6 :]
    x = stack(x_refs)
    gg_ref[...] = dot_tn(x, stack(dgate_refs)).astype(BF)
    gu_ref[...] = dot_tn(x, stack(dup_refs)).astype(BF)
    gd_ref[...] = dot_tn(stack(hidden_refs), stack(c_refs)).astype(BF)


def weighted(peers, me, routes_ref, gates_ref, place_ref, out, first):
    routes, gates = routes_ref[...], gates_ref[...]
    cp = place_ref.shape[0] // peers
    highs, lows = [], []
    for j in range(first, first + out.shape[0] // cp):
        place = place_ref[j * cp : (j + 1) * cp, :].astype(F32)
        gate = gate_row(routes, gates, me ^ j)
        high = gate.astype(BF).astype(F32)
        highs.append((place * high).astype(BF))
        lows.append((place * (gate - high)).astype(BF))
    return dot_tn(jnp.concatenate(highs, axis=0), out) + dot_tn(jnp.concatenate(lows, axis=0), out)


def mix_kernel(peers, me_ref, routes_ref, gates_ref, place_ref, *refs):
    out_refs, mixed_ref = refs[:-1], refs[-1]
    near = peers // 2
    mixed_ref[...] = weighted(
        peers, me_ref[0], routes_ref, gates_ref, place_ref, stack(out_refs), near
    )


def merge_kernel(peers, cap, me_ref, routes_ref, gates_ref, place_ref, far_ref, *refs):
    near = peers // 2
    out_refs, dx_refs, (mixed_ref, grad_ref, gates_out_ref) = refs[:near], refs[near:-3], refs[-3:]
    me = me_ref[0]
    routes, gates = routes_ref[...], gates_ref[...]
    cp = dx_refs[0].shape[0]
    mixed = weighted(peers, me, routes_ref, gates_ref, place_ref, stack(out_refs), 0)
    mixed_ref[...] = (far_ref[...] + mixed).astype(BF)
    grad_ref[...] = dot_tn(place_ref[...], stack(dx_refs)).astype(BF)
    total = jnp.zeros(gates.shape, F32)
    base = cap // 16 * 16
    at = cap - base
    for j in range(peers):
        place = place_ref[j * cp : (j + 1) * cp, :]
        found = dot(dx_refs[j][base:cp, :cp], place)
        value = found[at : at + 1] + found[at + 1 : at + 2] + found[at + 2 : at + 3]
        total = total + jnp.where(routes == (me ^ j), value, 0.0)
    gates_out_ref[...] = total / gates


def added(a, b):
    return (a.astype(F32) + b.astype(F32)).astype(BF)


def after(first, arrays):
    return lax.optimization_barrier((*first, *arrays))[len(first) :]


def paired(keep, send):
    return added(keep, swap(send, "dp", 1))


def both(pieces):
    return [*pieces, *(swap(piece, "dp", 1) for piece in pieces)]


def reduced(total, dp_count, pieces=1, first=()):
    bit = 2
    while bit < dp_count:
        arrived = swap(total, "dp", bit)
        bit *= 2
        if first and bit >= dp_count:
            (arrived,) = after(first, (arrived,))
        if bit >= dp_count:
            wide = total.shape[1] // pieces
            lanes = [slice(i * wide, (i + 1) * wide) for i in range(pieces)]
            return [added(total[:, part], arrived[:, part]) for part in lanes]
        total = added(total, arrived)


def shards(tokens, cotangent, routes, route_gates, gate_weight, up_weight, down_weight):
    peers = lax.axis_size("expert")
    near = peers // 2
    dp_count = lax.axis_size("dp")
    count, top = routes.shape
    width = tokens.shape[1]
    ff = gate_weight.shape[2]
    cap = 7 * count * top // (6 * peers)
    cp = -(-(cap + 3) // 16) * 16
    rows = near * cp
    gate_w, up_w, down_w = gate_weight[0], up_weight[0], down_weight[0]
    me = lax.axis_index("expert").astype(jnp.int32).reshape(1)
    half = (lax.axis_index("dp").astype(jnp.int32) & 1).reshape(1)
    routes_t, gates_t = routes.T, route_gates.T

    def sds(shape, dtype=BF):
        return jax.ShapeDtypeStruct(shape, dtype)

    part = sds((cp, width))
    *xs, place = call(
        functools.partial(pack_kernel, peers),
        "pack",
        [part] * peers + [sds((2 * rows, count))],
        (me, routes_t, tokens),
        flops=4 * rows * count * width,
    )
    cs = call(
        functools.partial(pack_cot_kernel, peers),
        "pack_cot",
        [part] * peers,
        (me, routes_t, gates_t, cotangent, place),
        flops=4 * rows * count * width,
    )
    weights = lax.optimization_barrier((gate_w, up_w, down_w, cs[0]))[:3]
    gate_w, up_w, down_w = call(
        load_kernel,
        "load",
        [sds(w.shape) for w in weights],
        weights,
        scalars=0,
        scratch=[pltpu.SemaphoreType.DMA((3,))],
    )
    xs = [xs[0]] + [swap(xs[j], "expert", j) for j in range(1, peers)]
    cs = [cs[0]] + [swap(cs[j], "expert", j) for j in range(1, peers)]
    work = 2 * rows * width * ff

    near_keep, near_send, far_keep, far_send = call(
        functools.partial(up_kernel, near),
        "up",
        [sds((rows // 2, 2 * ff))] * 4,
        (half, *xs[near:], *xs[:near], gate_w, up_w),
        flops=4 * work,
    )
    far_total = paired(far_keep, far_send)
    near_total = paired(near_keep, near_send)
    cs = after((far_total, near_total), (*cs[near:], *cs[:near]))
    cs = (*cs[near:], *cs[:near])
    (far_sum,) = reduced(far_total, dp_count)
    dh_keep, dh_send = call(
        functools.partial(back_kernel, near),
        "back",
        [sds((rows, ff))] * 2,
        (half, *cs[near:], *cs[:near], down_w),
        flops=2 * work,
    )
    dh_total = paired(dh_keep, dh_send)
    *outs, far_hidden, far_sums = call(
        functools.partial(out_kernel, near),
        "out",
        [part] * near + [sds((rows, ff)), sds((2, rows // 2, 2 * ff))],
        (half, far_sum, swap(far_sum, "dp", 1), down_w),
        flops=work,
    )
    near_sum = reduced(near_total, dp_count, NEAR_PIECES, NEAR_AFTER and (outs[0],))
    dh_sum = reduced(dh_total, dp_count, DH_PIECES, DH_AFTER and (outs[0],))
    near_sums, dh_sums = both(near_sum), both(dh_sum)

    *dxs, far_dgate, far_dup, dh = call(
        functools.partial(dx_kernel, near, cap),
        "dx",
        [part] * near + [sds((rows, ff))] * 2 + [sds((2, rows, ff))],
        (half, far_sums, far_hidden, gate_w, up_w, *dh_sums),
        scratch=[pltpu.VMEM((rows, 1), F32)],
        flops=DX_FLOPS * work,
    )
    dxs = [swap(dxs[j], "expert", near + j) for j in range(near)]
    outs = [swap(outs[j], "expert", near + j) for j in range(near)]
    (far_mixed,) = call(
        functools.partial(mix_kernel, peers),
        "mix",
        [sds((count, width), F32)],
        (me, routes_t, gates_t, place, *outs),
        flops=DX_FLOPS * rows * count * width,
    )
    (dh,) = after((far_mixed,), (dh,))
    produced = call(
        functools.partial(near_kernel, near, cap),
        "near",
        [part] * (2 * near) + [sds((rows, ff))] * 3,
        (half, dh, gate_w, up_w, down_w, *near_sums),
        scratch=[pltpu.VMEM((2, rows // 2, 2 * ff), BF), pltpu.VMEM((rows, 1), F32)],
        flops=DX_FLOPS * work,
    )
    near_outs, near_dxs, (near_hidden, near_dgate, near_dup) = (
        produced[:near],
        produced[near:peers],
        produced[peers:],
    )
    near_outs = [near_outs[0]] + [swap(near_outs[j], "expert", j) for j in range(1, near)]
    near_dxs = [near_dxs[0]] + [swap(near_dxs[j], "expert", j) for j in range(1, near)]

    grad_gate, grad_up, grad_down = call(
        functools.partial(grad_kernel, peers),
        "grads",
        [sds((width, ff))] * 2 + [sds((ff, width))],
        (*xs, *cs, near_hidden, far_hidden, near_dgate, far_dgate, near_dup, far_dup),
        scalars=0,
        flops=6 * work,
    )
    mixed, grad_tokens, gates_grad = call(
        functools.partial(merge_kernel, peers, cap),
        "merge",
        [sds((count, width))] * 2 + [sds((top, count), F32)],
        (me, routes_t, gates_t, place, far_mixed, *near_outs, *near_dxs, *dxs),
        flops=8 * rows * count * width,
    )
    return (mixed, grad_tokens, gates_grad.T, grad_gate[None], grad_up[None], grad_down[None])


def solution(mesh):
    in_specs = (
        P(("group", "expert"), "dp"),
        P(("group", "expert"), "dp"),
        P(("group", "expert"), None),
        P(("group", "expert"), None),
        P("expert", "dp", None),
        P("expert", "dp", None),
        P("expert", None, "dp"),
    )
    out_specs = (
        P(("group", "expert"), "dp"),
        P(("group", "expert"), "dp"),
        P(("group", "expert"), None),
        P(("group", "expert"), "dp", None),
        P(("group", "expert"), "dp", None),
        P(("group", "expert"), None, "dp"),
    )
    return jax.shard_map(shards, mesh=mesh, in_specs=in_specs, out_specs=out_specs, check_vma=False)
```

```python
import functools

import jax
import jax.numpy as jnp
from jax import lax
from jax.experimental import pallas as pl
from jax.experimental.pallas import tpu as pltpu
from jax.sharding import PartitionSpec as P

BF = jnp.bfloat16
F32 = jnp.float32
VMEM_BYTES = 40 * 1024 * 1024
NEAR_PIECES, DH_PIECES, DX_FLOPS = 2, 3, 0
NEAR_AFTER, DH_AFTER = True, True


def swap(block, axis, offset):
    count = lax.axis_size(axis)
    return lax.ppermute(block, axis, [(i, i ^ offset) for i in range(count)])


def dot(a, b):
    return lax.dot_general(a, b, (((1,), (0,)), ((), ())), preferred_element_type=F32)


def dot_nt(a, b):
    return lax.dot_general(a, b, (((1,), (1,)), ((), ())), preferred_element_type=F32)


def dot_tn(a, b):
    return lax.dot_general(a, b, (((0,), (0,)), ((), ())), preferred_element_type=F32)


def call(kernel, name, outs, args, scalars=1, hbm=0, scratch=(), flops=0):
    smem = pl.BlockSpec(memory_space=pltpu.SMEM)
    vmem = pl.BlockSpec(memory_space=pltpu.VMEM)
    moved = sum(a.size * a.dtype.itemsize for a in args) + sum(
        o.size * o.dtype.itemsize for o in outs
    )
    return pl.pallas_call(
        kernel,
        name=name,
        out_shape=outs,
        in_specs=[smem] * scalars
        + [pl.BlockSpec(memory_space=pltpu.HBM)] * hbm
        + [vmem] * (len(args) - scalars - hbm),
        out_specs=[vmem] * len(outs),
        scratch_shapes=list(scratch),
        compiler_params=pltpu.CompilerParams(vmem_limit_bytes=VMEM_BYTES),
        cost_estimate=pl.CostEstimate(flops=flops, bytes_accessed=moved, transcendentals=0),
    )(*args)


def chosen(routes, expert):
    return jnp.sum((routes == expert).astype(F32), axis=0, keepdims=True)


def gate_row(routes, gates, expert):
    return jnp.sum(jnp.where(routes == expert, gates, 0.0), axis=0, keepdims=True)


def pack_kernel(peers, me_ref, routes_ref, tokens_ref, *refs):
    x_refs, place_ref = refs[:peers], refs[peers]
    me = me_ref[0]
    count = routes_ref.shape[1]
    rows = x_refs[0].shape[0]
    earlier = (
        lax.broadcasted_iota(jnp.int32, (count, count), 0)
        < lax.broadcasted_iota(jnp.int32, (count, count), 1)
    ).astype(BF)
    slot = lax.broadcasted_iota(jnp.int32, (rows, count), 0)
    routes = routes_ref[...]
    taken = jnp.concatenate([chosen(routes, me ^ j) for j in range(peers)], axis=0)
    rank = dot(taken.astype(BF), earlier)
    rank = jnp.where(taken > 0.0, rank, -1.0).astype(jnp.int32)
    for j in range(peers):
        part = slice(j * rows, (j + 1) * rows)
        place_ref[part, :] = (slot == rank[j : j + 1]).astype(F32).astype(BF)
    tokens = tokens_ref[...]
    for j in reversed(range(peers)):
        part = slice(j * rows, (j + 1) * rows)
        x_refs[j][...] = dot(place_ref[part, :], tokens).astype(BF)


def pack_cot_kernel(peers, me_ref, routes_ref, gates_ref, cot_ref, place_ref, *c_refs):
    me = me_ref[0]
    rows = c_refs[0].shape[0]
    routes, gates = routes_ref[...], gates_ref[...]
    cot = cot_ref[...]
    for j in reversed(range(peers)):
        place = place_ref[j * rows : (j + 1) * rows, :]
        gate = gate_row(routes, gates, me ^ j)
        scale = jnp.sum(place.astype(F32) * gate, axis=1, keepdims=True)
        c_refs[j][...] = (dot(place, cot) * scale).astype(BF)


def load_kernel(*refs):
    count = (len(refs) - 1) // 2
    sem = refs[-1]
    copies = [pltpu.make_async_copy(refs[i], refs[count + i], sem.at[i]) for i in range(count)]
    for copy in copies:
        copy.start()
    for copy in copies:
        copy.wait()


def hand_out(half, y, start, lane, keep_ref, send_ref):
    rows = y.shape[0] // 2
    target = (slice(start, start + rows), slice(lane, lane + y.shape[1]))
    for h in range(2):

        @pl.when(half == h)
        def _():
            keep_ref[target] = y[h * rows : (h + 1) * rows]
            send_ref[target] = y[(1 - h) * rows : (2 - h) * rows]


def stack(refs, part=slice(None)):
    return jnp.concatenate([r[part, :] for r in refs], axis=0)


def up_kernel(near, half_ref, *refs):
    x_refs, (gate_ref, up_ref, near_keep, near_send, far_keep, far_send) = refs[:-6], refs[-6:]
    x_refs = x_refs[near:] + x_refs[:near]
    half = half_ref[0]
    x = stack(x_refs)
    rows = near * x_refs[0].shape[0]
    width = gate_ref.shape[1]
    for i, w_ref in enumerate((gate_ref, up_ref)):
        y = dot(x, w_ref[...]).astype(BF)
        hand_out(half, y[:rows], 0, i * width, near_keep, near_send)
        hand_out(half, y[rows:], 0, i * width, far_keep, far_send)


def back_kernel(near, half_ref, *refs):
    c_refs, (down_ref, keep_ref, send_ref) = refs[:-3], refs[-3:]
    c_refs = c_refs[near:] + c_refs[:near]
    half = half_ref[0]
    y = dot_nt(stack(c_refs), down_ref[...]).astype(BF)
    rows = near * c_refs[0].shape[0]
    hand_out(half, y[:rows], 0, 0, keep_ref, send_ref)
    hand_out(half, y[rows:], rows // 2, 0, keep_ref, send_ref)


def activate(g, u):
    return (g * jax.nn.sigmoid(g) * u).astype(BF)


def derive(g, u, dh):
    s = jax.nn.sigmoid(g)
    return (dh * u * s * (1.0 + g * (1.0 - s))).astype(BF), (dh * (g * s)).astype(BF)


def row_dots(hidden, dh):
    return jnp.sum(hidden.astype(F32) * dh, axis=1, keepdims=True)


def store_dx(cap, dx_ref, block, dots):
    cp = block.shape[0]
    lanes = 128 * (-(-cp // 128))
    row = lax.broadcasted_iota(jnp.int32, (cp, lanes), 0)
    eye = row == lax.broadcasted_iota(jnp.int32, (cp, lanes), 1)
    dots = jnp.sum(jnp.where(eye, dots, 0.0), axis=0, keepdims=True)
    high = dots.astype(BF).astype(F32)
    middle = (dots - high).astype(BF).astype(F32)
    low = dots - high - middle
    first = jnp.where(row == cap, high, block[:, :lanes])
    first = jnp.where(row == cap + 1, middle, first)
    first = jnp.where(row == cap + 2, low, first)
    dx_ref[:, :lanes] = first.astype(BF)
    dx_ref[:, lanes:] = block[:, lanes:].astype(BF)


def out_kernel(near, half_ref, mine_ref, other_ref, down_ref, *refs):
    out_refs, (hidden_ref, sums_ref) = refs[:near], refs[near:]
    half = half_ref[0]
    width = down_ref.shape[0]
    sums_ref[half] = mine_ref[...]
    sums_ref[1 - half] = other_ref[...]
    rows = mine_ref.shape[0]
    for h in range(2):
        g = sums_ref[h, :, :width].astype(F32)
        u = sums_ref[h, :, width:].astype(F32)
        hidden_ref[h * rows : (h + 1) * rows, :] = activate(g, u)
    out = dot(hidden_ref[...], down_ref[...]).astype(BF)
    cp = out_refs[0].shape[0]
    for j in range(near):
        out_refs[j][...] = out[j * cp : (j + 1) * cp]


def gather(half, refs, target_ref):
    count = len(refs) // 2
    wide = refs[0].shape[1]
    for i in range(count):
        target_ref[half, :, i * wide : (i + 1) * wide] = refs[i][...]
        target_ref[1 - half, :, i * wide : (i + 1) * wide] = refs[count + i][...]


def dx_rows(rows, width, source_ref, dh_ref, first, hidden_ref, dgate_ref, dup_ref, dot_ref):
    for h in range(2):
        part = slice(h * rows, (h + 1) * rows)
        g = source_ref[h, :, :width].astype(F32)
        u = source_ref[h, :, width:].astype(F32)
        dh = dh_ref[h, first : first + rows, :].astype(F32)
        dgate_ref[part, :], dup_ref[part, :] = derive(g, u, dh)
        dot_ref[part, :] = row_dots(hidden_ref[part, :], dh)


def dx_kernel(near, cap, half_ref, far_ref, hidden_ref, gate_ref, up_ref, *refs):
    dh_sums, refs = refs[: 2 * DH_PIECES], refs[2 * DH_PIECES :]
    dx_refs, (dgate_ref, dup_ref, dh_ref, dot_ref) = refs[:near], refs[near:]
    gather(half_ref[0], dh_sums, dh_ref)
    rows = far_ref.shape[1]
    dx_rows(rows, gate_ref.shape[1], far_ref, dh_ref, rows, hidden_ref, dgate_ref, dup_ref, dot_ref)
    dx = dot_nt(dgate_ref[...], gate_ref[...]) + dot_nt(dup_ref[...], up_ref[...])
    cp = dx_refs[0].shape[0]
    for j in range(near):
        part = slice(j * cp, (j + 1) * cp)
        store_dx(cap, dx_refs[j], dx[part], dot_ref[part, :])


def near_kernel(near, cap, half_ref, dh_ref, gate_ref, up_ref, down_ref, *refs):
    near_sums, refs = refs[: 2 * NEAR_PIECES], refs[2 * NEAR_PIECES :]
    out_refs, dx_refs, refs = refs[:near], refs[near : 2 * near], refs[2 * near :]
    hidden_ref, dgate_ref, dup_ref, near_ref, dot_ref = refs
    gather(half_ref[0], near_sums, near_ref)
    rows, width = near_ref.shape[1], gate_ref.shape[1]
    for h in range(2):
        g = near_ref[h, :, :width].astype(F32)
        u = near_ref[h, :, width:].astype(F32)
        hidden_ref[h * rows : (h + 1) * rows, :] = activate(g, u)
    dx_rows(rows, width, near_ref, dh_ref, 0, hidden_ref, dgate_ref, dup_ref, dot_ref)
    out = dot(hidden_ref[...], down_ref[...]).astype(BF)
    dx = dot_nt(dgate_ref[...], gate_ref[...]) + dot_nt(dup_ref[...], up_ref[...])
    cp = dx_refs[0].shape[0]
    for j in range(near):
        part = slice(j * cp, (j + 1) * cp)
        out_refs[j][...] = out[part]
        store_dx(cap, dx_refs[j], dx[part], dot_ref[part, :])


def grad_kernel(peers, *refs):
    x_refs, c_refs = refs[:peers], refs[peers : 2 * peers]
    hidden_refs, dgate_refs, dup_refs = (refs[2 * peers + 2 * i :][:2] for i in range(3))
    gg_ref, gu_ref, gd_ref = refs[2 * peers + 6 :]
    x = stack(x_refs)
    gg_ref[...] = dot_tn(x, stack(dgate_refs)).astype(BF)
    gu_ref[...] = dot_tn(x, stack(dup_refs)).astype(BF)
    gd_ref[...] = dot_tn(stack(hidden_refs), stack(c_refs)).astype(BF)


def weighted(peers, me, routes_ref, gates_ref, place_ref, out, first):
    routes, gates = routes_ref[...], gates_ref[...]
    cp = place_ref.shape[0] // peers
    highs, lows = [], []
    for j in range(first, first + out.shape[0] // cp):
        place = place_ref[j * cp : (j + 1) * cp, :].astype(F32)
        gate = gate_row(routes, gates, me ^ j)
        high = gate.astype(BF).astype(F32)
        highs.append((place * high).astype(BF))
        lows.append((place * (gate - high)).astype(BF))
    return dot_tn(jnp.concatenate(highs, axis=0), out) + dot_tn(jnp.concatenate(lows, axis=0), out)


def mix_kernel(peers, me_ref, routes_ref, gates_ref, place_ref, *refs):
    out_refs, mixed_ref = refs[:-1], refs[-1]
    near = peers // 2
    mixed_ref[...] = weighted(
        peers, me_ref[0], routes_ref, gates_ref, place_ref, stack(out_refs), near
    )


def far_kernel(place_ref, *refs):
    dx_refs, grad_ref = refs[:-1], refs[-1]
    grad_ref[...] = dot_tn(place_ref[place_ref.shape[0] // 2 :, :], stack(dx_refs))


def merge_kernel(peers, cap, me_ref, routes_ref, gates_ref, place_ref, far_ref, far_grad_ref, *refs):
    near = peers // 2
    out_refs, dx_refs, (mixed_ref, grad_ref, gates_out_ref) = refs[:near], refs[near:-3], refs[-3:]
    me = me_ref[0]
    routes, gates = routes_ref[...], gates_ref[...]
    cp = dx_refs[0].shape[0]
    mixed = weighted(peers, me, routes_ref, gates_ref, place_ref, stack(out_refs), 0)
    mixed_ref[...] = (far_ref[...] + mixed).astype(BF)
    near_dx = dot_tn(place_ref[: near * cp, :], stack(dx_refs[:near]))
    grad_ref[...] = (far_grad_ref[...] + near_dx).astype(BF)
    total = jnp.zeros(gates.shape, F32)
    base = cap // 16 * 16
    at = cap - base
    for j in range(peers):
        place = place_ref[j * cp : (j + 1) * cp, :]
        found = dot(dx_refs[j][base:cp, :cp], place)
        value = found[at : at + 1] + found[at + 1 : at + 2] + found[at + 2 : at + 3]
        total = total + jnp.where(routes == (me ^ j), value, 0.0)
    gates_out_ref[...] = total / gates


def added(a, b):
    return (a.astype(F32) + b.astype(F32)).astype(BF)


def after(first, arrays):
    return lax.optimization_barrier((*first, *arrays))[len(first) :]


def paired(keep, send):
    return added(keep, swap(send, "dp", 1))


def both(pieces):
    return [*pieces, *(swap(piece, "dp", 1) for piece in pieces)]


def reduced(total, dp_count, pieces=1, first=()):
    bit = 2
    while bit < dp_count:
        arrived = swap(total, "dp", bit)
        bit *= 2
        if first and bit >= dp_count:
            (arrived,) = after(first, (arrived,))
        if bit >= dp_count:
            wide = total.shape[1] // pieces
            lanes = [slice(i * wide, (i + 1) * wide) for i in range(pieces)]
            return [added(total[:, part], arrived[:, part]) for part in lanes]
        total = added(total, arrived)


def shards(tokens, cotangent, routes, route_gates, gate_weight, up_weight, down_weight):
    peers = lax.axis_size("expert")
    near = peers // 2
    dp_count = lax.axis_size("dp")
    count, top = routes.shape
    width = tokens.shape[1]
    ff = gate_weight.shape[2]
    cap = 7 * count * top // (6 * peers)
    cp = -(-(cap + 3) // 16) * 16
    rows = near * cp
    gate_w, up_w, down_w = gate_weight[0], up_weight[0], down_weight[0]
    me = lax.axis_index("expert").astype(jnp.int32).reshape(1)
    half = (lax.axis_index("dp").astype(jnp.int32) & 1).reshape(1)
    routes_t, gates_t = routes.T, route_gates.T

    def sds(shape, dtype=BF):
        return jax.ShapeDtypeStruct(shape, dtype)

    part = sds((cp, width))
    *xs, place = call(
        functools.partial(pack_kernel, peers),
        "pack",
        [part] * peers + [sds((2 * rows, count))],
        (me, routes_t, tokens),
        flops=4 * rows * count * width,
    )
    cs = call(
        functools.partial(pack_cot_kernel, peers),
        "pack_cot",
        [part] * peers,
        (me, routes_t, gates_t, cotangent, place),
        flops=4 * rows * count * width,
    )
    weights = lax.optimization_barrier((gate_w, up_w, down_w, cs[0]))[:3]
    gate_w, up_w, down_w = call(
        load_kernel,
        "load",
        [sds(w.shape) for w in weights],
        weights,
        scalars=0,
        scratch=[pltpu.SemaphoreType.DMA((3,))],
    )
    xs = [xs[0]] + [swap(xs[j], "expert", j) for j in range(1, peers)]
    cs = [cs[0]] + [swap(cs[j], "expert", j) for j in range(1, peers)]
    work = 2 * rows * width * ff

    near_keep, near_send, far_keep, far_send = call(
        functools.partial(up_kernel, near),
        "up",
        [sds((rows // 2, 2 * ff))] * 4,
        (half, *xs[near:], *xs[:near], gate_w, up_w),
        flops=4 * work,
    )
    far_total = paired(far_keep, far_send)
    near_total = paired(near_keep, near_send)
    cs = after((far_total, near_total), (*cs[near:], *cs[:near]))
    cs = (*cs[near:], *cs[:near])
    (far_sum,) = reduced(far_total, dp_count)
    dh_keep, dh_send = call(
        functools.partial(back_kernel, near),
        "back",
        [sds((rows, ff))] * 2,
        (half, *cs[near:], *cs[:near], down_w),
        flops=2 * work,
    )
    dh_total = paired(dh_keep, dh_send)
    *outs, far_hidden, far_sums = call(
        functools.partial(out_kernel, near),
        "out",
        [part] * near + [sds((rows, ff)), sds((2, rows // 2, 2 * ff))],
        (half, far_sum, swap(far_sum, "dp", 1), down_w),
        flops=work,
    )
    near_sum = reduced(near_total, dp_count, NEAR_PIECES, NEAR_AFTER and (outs[0],))
    dh_sum = reduced(dh_total, dp_count, DH_PIECES, DH_AFTER and (outs[0],))
    near_sums, dh_sums = both(near_sum), both(dh_sum)

    *dxs, far_dgate, far_dup, dh = call(
        functools.partial(dx_kernel, near, cap),
        "dx",
        [part] * near + [sds((rows, ff))] * 2 + [sds((2, rows, ff))],
        (half, far_sums, far_hidden, gate_w, up_w, *dh_sums),
        scratch=[pltpu.VMEM((rows, 1), F32)],
        flops=DX_FLOPS * work,
    )
    dxs = [swap(dxs[j], "expert", near + j) for j in range(near)]
    outs = [swap(outs[j], "expert", near + j) for j in range(near)]
    (far_mixed,) = call(
        functools.partial(mix_kernel, peers),
        "mix",
        [sds((count, width), F32)],
        (me, routes_t, gates_t, place, *outs),
        flops=DX_FLOPS * rows * count * width,
    )
    (dh,) = after((far_mixed,), (dh,))
    produced = call(
        functools.partial(near_kernel, near, cap),
        "near",
        [part] * (2 * near) + [sds((rows, ff))] * 3,
        (half, dh, gate_w, up_w, down_w, *near_sums),
        scratch=[pltpu.VMEM((2, rows // 2, 2 * ff), BF), pltpu.VMEM((rows, 1), F32)],
        flops=DX_FLOPS * work,
    )
    near_outs, near_dxs, (near_hidden, near_dgate, near_dup) = (
        produced[:near],
        produced[near:peers],
        produced[peers:],
    )
    near_outs = [near_outs[0]] + [swap(near_outs[j], "expert", j) for j in range(1, near)]
    near_dxs = [near_dxs[0]] + [swap(near_dxs[j], "expert", j) for j in range(1, near)]

    grad_gate, grad_up, grad_down = call(
        functools.partial(grad_kernel, peers),
        "grads",
        [sds((width, ff))] * 2 + [sds((ff, width))],
        (*xs, *cs, near_hidden, far_hidden, near_dgate, far_dgate, near_dup, far_dup),
        scalars=0,
        flops=6 * work,
    )
    (far_grad,) = call(
        far_kernel,
        "far",
        [sds((count, width), F32)],
        (place, *dxs),
        scalars=0,
        flops=0,
    )
    mixed, grad_tokens, gates_grad = call(
        functools.partial(merge_kernel, peers, cap),
        "merge",
        [sds((count, width))] * 2 + [sds((top, count), F32)],
        (me, routes_t, gates_t, place, far_mixed, far_grad, *near_outs, *near_dxs, *dxs),
        flops=8 * rows * count * width,
    )
    return (mixed, grad_tokens, gates_grad.T, grad_gate[None], grad_up[None], grad_down[None])


def solution(mesh):
    in_specs = (
        P(("group", "expert"), "dp"),
        P(("group", "expert"), "dp"),
        P(("group", "expert"), None),
        P(("group", "expert"), None),
        P("expert", "dp", None),
        P("expert", "dp", None),
        P("expert", None, "dp"),
    )
    out_specs = (
        P(("group", "expert"), "dp"),
        P(("group", "expert"), "dp"),
        P(("group", "expert"), None),
        P(("group", "expert"), "dp", None),
        P(("group", "expert"), "dp", None),
        P(("group", "expert"), None, "dp"),
    )
    return jax.shard_map(shards, mesh=mesh, in_specs=in_specs, out_specs=out_specs, check_vma=False)
```
